256 devices in a mesh: group: 8 (over z), seq: 2 (over core), req: 16 (over y, x).
Axes of the slice: x: 4, y: 4, z: 8, core: 2. Of those that a mesh axis runs over, the one named last changes fastest.
Arguments:
- queries: bfloat16 [2, 128, 4, 128, 192], P(None, ('group', 'req')), may hold values from -8 to 8
- w_absorb_k: bfloat16 [2, 128, 128, 512], P(None, 'req', None, 'seq'), may hold values from -0.5 to 0.5
- w_absorb_v: bfloat16 [2, 128, 512, 128], P(None, 'req', 'seq'), may hold values from -1.1953125 to 1.1953125
- prefill_pages: bfloat16 [16, 16, 2, 16, 64, 576], P(('group', 'seq'), 'req'), may hold values from -8 to 8
- send_to: int32 [16, 16, 16], P(('group', 'seq'), 'req'), may hold values from 0 to 15, each once within a row
- slot_of: int32 [16, 16, 16], P(('group', 'seq'), 'req'), may hold values from 0 to 15, each once within a row
- lengths: int32 [128], P(('group', 'req')), may hold values from 1 to 2048, 131072 in all
- new_latents: bfloat16 [2, 128, 4, 576], P(None, ('group', 'req')), may hold values from -6 to 6
Outputs:
- attn_out: bfloat16 [2, 128, 4, 128, 128], P(None, 'group', None, 'req')
The draws below stay inside these ranges and needn't reach their ends.
Inputs may be any that keep to these rules, and one draw needn't show every extreme that they name: For each prefill device and request column (r), send_to is a permutation of the 16 holders of that column (numbered group-major): each prefill device holds exactly one page for each holder. For each holder and request column (r), slot_of is a permutation: the page from prefill device p fills page slot slot_of[p] of the holder's block.
All inputs are finite; a program needn't handle non-finite values. No bound on the sum of `lengths` on one device may be relied on, other than what follows from the above.
Results may differ from the reference program's by a relative error of at most 0.0075.
Values may be sent and summed in bfloat16 or wider, within the bound.
No kernel may reach another device: no remote copies, remote signals or barrier semaphores. Data moves between devices by JAX's collectives and lax.ppermute only.
A program may use at most 192 MiB of HBM per device.

```python
import math
import jax
import jax.numpy as jnp
import numpy as np
from jax import lax

KV_RANK = 512
ROPE = 64
NOPE = 128
VDIM = 128
HEADS = 128
LAYERS = 2
STEPS = 4
CT = 1024
PLANE = 16
PAGE = 64
LMAX = 2048
REQS = 128
N_SEQ = 2
N_REQ = 16


def draw_queries(key, part):
    key = jax.random.fold_in(key, 3)
    shape = (LAYERS, REQS, STEPS, HEADS, NOPE + ROPE)
    first = jax.random.fold_in(key, 0)
    values = jnp.clip(jax.random.normal(first, shape, jnp.float32), -6.0, 6.0)
    return values.astype(jnp.bfloat16)


def draw_prefill_pages(key, part):
    key = jax.random.fold_in(key, 7)
    shape = (PLANE, N_REQ, LAYERS, PLANE, PAGE, KV_RANK + ROPE)
    first = jax.random.fold_in(key, 0)
    values = jnp.clip(jax.random.normal(first, shape, jnp.float32), -6.0, 6.0)
    return values.astype(jnp.bfloat16)


def levels(key, extent, shards, least, largest):
    def one(position, parts):
        heights = jax.random.uniform(jax.random.fold_in(jax.random.fold_in(key, 6), position), (parts,), jnp.float32, least / len(shards), largest / len(shards))
        return jnp.repeat(jnp.exp(heights), extent[position] // parts).reshape((-1,) + (1,) * (len(extent) - position - 1))

    factor_of = one(*shards[0])
    for cut in shards[1:]:
        factor_of = factor_of * one(*cut)
    return factor_of


def profile(number_of, total, most, skew):
    weights = [(1 << 20) // math.isqrt(standing ** skew) + 1 for standing in range(2, number_of + 1)]
    rest, given = total - most - (number_of - 1), [1] * (number_of - 1)
    while rest > 0:
        free = [i for i in range(number_of - 1) if given[i] < most]
        pool, left = sum([weights[i] for i in free]), rest
        for i in free:
            extra = min(most - given[i], max(1, left * weights[i] // pool), rest)
            given[i] = given[i] + extra
            rest = rest - extra
    return np.array([most] + given)


def ragged_sizes(stream_key, count, total, reach, skew):
    if count == 2:
        one = jax.random.randint(stream_key, (), max(1, total - reach), min(reach, total - 1) + 1)
        return jnp.stack([one, total - one])
    sizes = jnp.asarray(profile(count, total, reach, skew), jnp.int32)
    couples = (count - 1) // 2
    donor, receiver = sizes[1:1 + 2 * couples:2], sizes[2:2 + 2 * couples:2]
    margin = jnp.minimum(donor - 1, reach - receiver)
    moved = jax.random.randint(jax.random.fold_in(stream_key, 1), (couples,), 0, 1 << 20) % (margin + 1)
    sizes = sizes.at[1:1 + 2 * couples:2].set(donor - moved).at[2:2 + 2 * couples:2].set(receiver + moved)
    return sizes[jax.random.permutation(jax.random.fold_in(stream_key, 2), count)]


def scatter_about(own_key, extent, deviation, bound, cuts=(), kind=jnp.bfloat16):
    level = levels(own_key, extent, cuts, -0.22, 0.18) if cuts else 1.0
    drawn = jax.random.normal(own_key, extent, jnp.float32) * deviation * level
    return jnp.minimum(jnp.maximum(drawn, -bound), bound).astype(kind)


def setup_inputs(seed: int = 0) -> dict:
    seeds = jax.random.split(jax.random.key(seed), 9)
    queries = draw_queries(jax.random.fold_in(seeds[8], 71), 0)
    w_absorb_k = scatter_about(seeds[1], (LAYERS, HEADS, NOPE, KV_RANK), NOPE ** -0.5, 0.5, ((1, 16), (3, 2)))
    w_absorb_v = scatter_about(seeds[2], (LAYERS, HEADS, KV_RANK, VDIM), 0.2, 1.1953125, ((1, 16), (2, 2)))
    prefill_pages = draw_prefill_pages(jax.random.fold_in(seeds[8], 71), 0)
    send_to = jax.vmap(lambda own: jax.random.permutation(own, PLANE))(jax.random.split(seeds[4], PLANE * N_REQ)).reshape((PLANE, N_REQ, PLANE)).astype(jnp.int32)
    slot_of = jax.vmap(lambda own: jax.random.permutation(own, PLANE))(jax.random.split(seeds[5], PLANE * N_REQ)).reshape((PLANE, N_REQ, PLANE)).astype(jnp.int32)
    lengths = ragged_sizes(seeds[6], REQS, REQS * LMAX // 2, LMAX, 2).astype(jnp.int32)
    new_latents = scatter_about(seeds[7], (LAYERS, REQS, STEPS, KV_RANK + ROPE), 1.0, 6.0, ((1, 128),))
    return dict(queries=queries, w_absorb_k=w_absorb_k, w_absorb_v=w_absorb_v, prefill_pages=prefill_pages, send_to=send_to, slot_of=slot_of, lengths=lengths, new_latents=new_latents)


empty_score = -1e+30

def request_cache(prefill_pages, which_page, slot_of, request):
    group_index = request // N_REQ
    column = request % N_REQ
    column_pages = jnp.take(prefill_pages, column, axis=1)
    column_which = jnp.take(which_page, column, axis=1)
    column_slots = jnp.take(slot_of, column, axis=1)
    holders = group_index * N_SEQ + jnp.arange(N_SEQ, dtype=jnp.int32)

    def pick_page(page_group, page_index):
        return jnp.take(page_group, page_index, axis=1)

    def holder_cache(holder):
        page_index = jnp.take(column_which, holder, axis=1).astype(jnp.int32)
        received = jax.vmap(pick_page)(column_pages, page_index)
        sources = jnp.argsort(jnp.take(column_slots, holder, axis=0)).astype(jnp.int32)
        placed = jnp.take(received, sources, axis=0)
        return jnp.transpose(placed, (1, 0, 2, 3)).reshape(LAYERS, CT, KV_RANK + ROPE)
    return jax.vmap(holder_cache)(holders)

def request_output(queries_one, new_one, length, caches, w_absorb_k, w_absorb_v):
    scale = 1.0 / math.sqrt(NOPE + ROPE)
    positions = jnp.arange(N_SEQ, dtype=jnp.int32)[:, None] * CT + jnp.arange(CT, dtype=jnp.int32)[None, :]
    block_live = (positions < length)[:, None, None, :]
    step_index = jnp.arange(STEPS, dtype=jnp.int32)
    new_mask = (step_index[None, :] <= step_index[:, None])[:, None, :]
    outputs = []
    for layer_index in range(LAYERS):
        query_nope = queries_one[layer_index, :, :, :NOPE].astype(jnp.float32)
        latent_query = jnp.einsum('thd,hdc->thc', query_nope, w_absorb_k[layer_index].astype(jnp.float32)).astype(jnp.bfloat16)
        full_query = jnp.concatenate([latent_query, queries_one[layer_index, :, :, NOPE:]], axis=-1).astype(jnp.float32)
        block_keys = caches[:, layer_index].astype(jnp.float32)
        new_keys = new_one[layer_index].astype(jnp.float32)
        block_scores = jnp.einsum('thw,bkw->bthk', full_query, block_keys) * scale
        new_scores = jnp.einsum('thw,uw->thu', full_query, new_keys) * scale
        block_peak = lax.optimization_barrier(jnp.max(jnp.where(block_live, block_scores, empty_score), axis=-1))
        new_peak = lax.optimization_barrier(jnp.max(jnp.where(new_mask, new_scores, empty_score), axis=-1))
        block_peak = block_peak.at[0].set(jnp.maximum(block_peak[0], new_peak))
        block_weights = jnp.where(block_live, jnp.exp(block_scores - block_peak[..., None]), 0.0).astype(jnp.bfloat16)
        new_weights = jnp.where(new_mask, jnp.exp(new_scores - block_peak[0][..., None]), 0.0).astype(jnp.bfloat16)
        block_total = lax.optimization_barrier(jnp.sum(block_weights.astype(jnp.float32), axis=-1))
        block_total = block_total.at[0].add(lax.optimization_barrier(jnp.sum(new_weights.astype(jnp.float32), axis=-1)))
        block_sum = jnp.einsum('bthk,bkc->bthc', block_weights.astype(jnp.float32), block_keys[..., :KV_RANK])
        block_sum = block_sum.at[0].add(jnp.einsum('thu,uc->thc', new_weights.astype(jnp.float32), new_keys[:, :KV_RANK]))
        overall = lax.optimization_barrier(jnp.max(block_peak, axis=0))
        factor = jnp.exp(block_peak - overall[None])
        numerator = lax.optimization_barrier(jnp.sum(block_sum * factor[..., None], axis=0))
        denominator = lax.optimization_barrier(jnp.sum(block_total * factor, axis=0))
        latent_out = (numerator / denominator[..., None]).astype(jnp.bfloat16)
        head_out = jnp.einsum('thc,hcv->thv', latent_out.astype(jnp.float32), w_absorb_v[layer_index].astype(jnp.float32))
        outputs.append(head_out.astype(jnp.bfloat16))
    return jnp.stack(outputs)

def reference(queries, w_absorb_k, w_absorb_v, prefill_pages, send_to, slot_of, lengths, new_latents):
    which_page = jnp.argsort(send_to, axis=-1).astype(jnp.int32)

    def one_request(request):
        caches = request_cache(prefill_pages, which_page, slot_of, request)
        return request_output(jnp.take(queries, request, axis=1), jnp.take(new_latents, request, axis=1), jnp.take(lengths, request), caches, w_absorb_k, w_absorb_v)
    results = lax.map(one_request, jnp.arange(REQS, dtype=jnp.int32))
    return jnp.transpose(results, (1, 0, 2, 3, 4))
```

```python
import math

import jax
import jax.numpy as jnp
from jax import lax
from jax.experimental import pallas as pl
from jax.experimental.pallas import tpu as pltpu
from jax.sharding import PartitionSpec as P

KV_RANK = 512
ROPE = 64
NOPE = 128
HEADS_PER = 8
STEPS = 4
PAGE = 64
SIDE = 4
SRC = 16
PAIR_ROWS = 2 * PAGE + 16
DEAD = -1e30
SCALE = 1.0 / math.sqrt(NOPE + ROPE)


def send_kernel(page_of, pages, out, held, packed, in_sem, lat_sem, rope_sem):
    def fetch(dest, half):
        chip, layer = dest // 2, dest % 2
        index = dest * 2 + half
        return pltpu.make_async_copy(
            pages.at[layer, page_of[chip * 2 + half]], held.at[index], in_sem.at[index]
        )

    def latents(dest, half):
        index = dest * 2 + half
        return pltpu.make_async_copy(
            held.at[index, :, pl.ds(0, KV_RANK)],
            out.at[dest, pl.ds(half * PAGE, PAGE)],
            lat_sem.at[index],
        )

    def ropes(dest):
        return pltpu.make_async_copy(
            packed.at[dest], out.at[dest, pl.ds(2 * PAGE, 16)], rope_sem.at[dest]
        )

    for dest in range(SRC):
        for half in range(2):
            fetch(dest, half).start()
    for dest in range(SRC):
        for half in range(2):
            fetch(dest, half).wait()
            latents(dest, half).start()
        groups = [
            held[dest * 2 + half, 16 * k : 16 * k + 16, KV_RANK:]
            for half in range(2)
            for k in range(PAGE // 16)
        ]
        packed[dest] = jnp.concatenate(groups, axis=1)
        ropes(dest).start()
    for dest in range(SRC):
        for half in range(2):
            latents(dest, half).wait()
        ropes(dest).wait()


def gather_pages(page_of, pages):
    return pl.pallas_call(
        send_kernel,
        out_shape=jax.ShapeDtypeStruct((SRC, PAIR_ROWS, KV_RANK), jnp.bfloat16),
        in_specs=[
            pl.BlockSpec(memory_space=pltpu.SMEM),
            pl.BlockSpec(memory_space=pl.ANY),
        ],
        out_specs=pl.BlockSpec(memory_space=pl.ANY),
        scratch_shapes=[
            pltpu.VMEM((2 * SRC, PAGE, KV_RANK + ROPE), jnp.bfloat16),
            pltpu.VMEM((SRC, 16, KV_RANK), jnp.bfloat16),
            pltpu.SemaphoreType.DMA((2 * SRC,)),
            pltpu.SemaphoreType.DMA((2 * SRC,)),
            pltpu.SemaphoreType.DMA((SRC,)),
        ],
        compiler_params=pltpu.CompilerParams(vmem_limit_bytes=24 << 20),
        cost_estimate=pl.CostEstimate(flops=0, bytes_accessed=5 << 20, transcendentals=0),
    )(page_of, pages)


def attend_kernel(order, q_lat, q_rope, pages, bias, new_lat, new_rope, out, ropes, scores):
    contract = (((1,), (1,)), ((), ()))

    def dot(a, b):
        return lax.dot_general(a, b, contract, preferred_element_type=jnp.float32)

    rows = q_lat.shape[0]
    for p in range(SRC):
        for k in range(8):
            ropes[p * 128 + 16 * k : p * 128 + 16 * k + 16, :] = pages[
                p, 2 * PAGE : PAIR_ROWS, ROPE * k : ROPE * k + ROPE
            ]
    ql, qr = q_lat[...], q_rope[...]
    step = lax.rem(lax.broadcasted_iota(jnp.int32, (rows, 16), 0) // HEADS_PER, STEPS)
    key = lax.broadcasted_iota(jnp.int32, (rows, 16), 1)
    fresh = (dot(ql, new_lat[...]) + dot(qr, new_rope[...])) * SCALE
    fresh = jnp.where(key <= step, fresh, DEAD)
    peak = jnp.max(fresh, axis=1, keepdims=True)
    chunk = 256
    for n in range(SRC // 2):
        part = slice(n * chunk, (n + 1) * chunk)
        lat = pages[2 * n : 2 * n + 2, : 2 * PAGE, :].reshape(chunk, KV_RANK)
        s = (dot(ql, lat) + dot(qr, ropes[part, :])) * SCALE
        s = jnp.where(bias[:, part] > 0.0, s, DEAD)
        scores[:, part] = s
        peak = jnp.maximum(peak, jnp.max(s, axis=1, keepdims=True))
    weight = jnp.exp(fresh - peak).astype(jnp.bfloat16)
    total = jnp.sum(weight.astype(jnp.float32), axis=1, keepdims=True)
    summed = jnp.dot(weight, new_lat[...], preferred_element_type=jnp.float32)
    for n in range(SRC // 2):
        part = slice(n * chunk, (n + 1) * chunk)
        lat = pages[2 * n : 2 * n + 2, : 2 * PAGE, :].reshape(chunk, KV_RANK)
        weight = jnp.exp(scores[:, part] - peak).astype(jnp.bfloat16)
        total = total + jnp.sum(weight.astype(jnp.float32), axis=1, keepdims=True)
        summed = summed + jnp.dot(weight, lat, preferred_element_type=jnp.float32)
    result = (summed / total).astype(jnp.bfloat16)
    block = HEADS_PER * STEPS
    for j in range(SRC):
        out[order[j]] = result[j * block : (j + 1) * block]


def attend(order, q_lat, q_rope, pages, bias, new_lat, new_rope):
    block = HEADS_PER * STEPS
    vmem = pl.BlockSpec(memory_space=pltpu.VMEM)
    rows = q_lat.shape[0]
    return pl.pallas_call(
        attend_kernel,
        out_shape=jax.ShapeDtypeStruct((SRC, block, KV_RANK), jnp.bfloat16),
        in_specs=[pl.BlockSpec(memory_space=pltpu.SMEM)] + [vmem] * 6,
        out_specs=vmem,
        scratch_shapes=[
            pltpu.VMEM((SRC * 2 * PAGE, ROPE), jnp.bfloat16),
            pltpu.VMEM((rows, SRC * 2 * PAGE), jnp.float32),
        ],
        compiler_params=pltpu.CompilerParams(vmem_limit_bytes=40 << 20),
        cost_estimate=pl.CostEstimate(
            flops=2 * rows * 2048 * 1088, bytes_accessed=4 << 20, transcendentals=rows * 2048
        ),
    )(order, q_lat, q_rope, pages, bias, new_lat, new_rope)


def shifted(value, dy, dx):
    pairs = [
        (y * SIDE + x, ((y + dy) % SIDE) * SIDE + (x + dx) % SIDE)
        for y in range(SIDE)
        for x in range(SIDE)
    ]
    return lax.ppermute(value, "req", pairs)


def exchange(value):
    columns = [value[:, 0]] + [shifted(value[:, d], 0, d) for d in range(1, SIDE)]
    rows = jnp.stack(columns, axis=1)
    return jnp.stack([rows[0]] + [shifted(rows[d], d, 0) for d in range(1, SIDE)])


def swapped(value):
    return lax.ppermute(value, "seq", [(0, 1), (1, 0)])


def pick(value, index):
    return lax.dynamic_index_in_dim(value, index, 0, keepdims=False)


def shards(queries, w_absorb_k, w_absorb_v, prefill_pages, send_to, slot_of, lengths, new_latents):
    layer = lax.axis_index("seq")
    place = lax.axis_index("req")
    py, px = place // SIDE, place % SIDE
    length = lengths[0]
    numbers = jnp.arange(SRC, dtype=jnp.int32)

    page_of = jnp.sum(
        jnp.where(send_to[0, 0][None, :] == numbers[:, None], numbers[None, :], 0), axis=1
    )
    sent = gather_pages(page_of, prefill_pages[0, 0])
    pages = lax.all_to_all(sent, ("group", "seq"), split_axis=0, concat_axis=0, tiled=True)

    forward = ((py + numbers // SIDE) % SIDE) * SIDE + (px + numbers % SIDE) % SIDE
    backward = ((py - numbers // SIDE) % SIDE) * SIDE + (px - numbers % SIDE) % SIDE

    own_k, other_k = pick(w_absorb_k, layer), swapped(pick(w_absorb_k, 1 - layer))
    weight_k = jnp.where(
        layer == 0,
        jnp.concatenate([own_k, other_k], axis=2),
        jnp.concatenate([other_k, own_k], axis=2),
    )
    own_v, other_v = pick(w_absorb_v, layer), swapped(pick(w_absorb_v, 1 - layer))
    weight_v = jnp.where(
        layer == 0,
        jnp.concatenate([own_v, other_v], axis=1),
        jnp.concatenate([other_v, own_v], axis=1),
    )

    own = pick(queries, layer)[0].reshape(STEPS, SRC, HEADS_PER, NOPE + ROPE).transpose(1, 0, 2, 3)
    own = jnp.take(own, forward, axis=0, mode="clip")
    grid = (SIDE, SIDE, STEPS, HEADS_PER)
    heads = exchange(own[..., :NOPE].reshape(grid + (NOPE,)))
    latent = jnp.einsum(
        "yxthd,hdc->yxthc", heads, weight_k, preferred_element_type=jnp.float32
    ).astype(jnp.bfloat16)
    turned = (-jnp.arange(SIDE)) % SIDE
    back = exchange(latent[turned][:, turned])[turned][:, turned]
    rows = SRC * STEPS * HEADS_PER
    q_lat = back.reshape(rows, KV_RANK)
    q_rope = own[..., NOPE:].reshape(rows, ROPE)

    other_slot = swapped(slot_of[0, 0])
    slots = jnp.where(
        layer == 0, jnp.stack([slot_of[0, 0], other_slot]), jnp.stack([other_slot, slot_of[0, 0]])
    )
    starts = jnp.arange(2, dtype=jnp.int32)[None, :] * 1024 + slots.T * PAGE
    live = starts[:, :, None] + jnp.arange(PAGE, dtype=jnp.int32) < length
    bias = live.reshape(1, SRC * 2 * PAGE).astype(jnp.float32)
    fresh = jnp.pad(pick(new_latents, layer)[0], ((0, 16 - STEPS), (0, 0)))
    latent_out = attend(
        forward, q_lat, q_rope, pages, bias, fresh[:, :KV_RANK], fresh[:, KV_RANK:]
    )

    latent_heads = lax.all_to_all(latent_out, "req", split_axis=0, concat_axis=0, tiled=True)
    head_out = jnp.einsum(
        "rthc,hcv->rthv",
        latent_heads.reshape(SRC, STEPS, HEADS_PER, KV_RANK),
        weight_v,
        preferred_element_type=jnp.float32,
    ).astype(jnp.bfloat16)
    return lax.all_gather(head_out, "seq", axis=0)


def solution(mesh):
    in_specs = (
        P(None, ("group", "req"), None, None, None),
        P(None, "req", None, "seq"),
        P(None, "req", "seq", None),
        P(("group", "seq"), "req", None, None, None, None),
        P(("group", "seq"), "req", None),
        P(("group", "seq"), "req", None),
        P(("group", "req")),
        P(None, ("group", "req"), None, None),
    )
    out_specs = P(None, "group", None, "req", None)
    return jax.shard_map(shards, mesh=mesh, in_specs=in_specs, out_specs=out_specs, check_vma=False)
```

```python
import functools
import math

import jax
import jax.numpy as jnp
from jax import lax
from jax.experimental import pallas as pl
from jax.experimental.pallas import tpu as pltpu
from jax.sharding import PartitionSpec as P

KV_RANK = 512
ROPE = 64
NOPE = 128
VDIM = 128
HEADS_PER = 8
STEPS = 4
PAGE = 64
PEERS = 16
BLOCK_KEYS = 1024
PAIR = 2 * PAGE
PAIR_ROWS = PAIR + 16
BLOCK = HEADS_PER * STEPS
ROWS = PEERS * BLOCK
HALF = KV_RANK // 2
DEAD = -1e30
SCALE = 1.0 / math.sqrt(NOPE + ROPE)
TO_LOG2 = SCALE * math.log2(math.e)
SIDE = 4
VMEM = pl.BlockSpec(memory_space=pltpu.VMEM)
SMEM = pl.BlockSpec(memory_space=pltpu.SMEM)
ANY = pl.BlockSpec(memory_space=pl.ANY)


def send_kernel(send_to, pages, out, target_of, page_of, held, packed, target_sem, in_sem, lat_sem, rope_sem):
    targets = pltpu.make_async_copy(send_to, target_of, target_sem)
    targets.start()

    def fetch(layer):
        return pltpu.make_async_copy(pages.at[layer], held.at[layer], in_sem.at[layer])

    def latents(dest, half):
        index = dest * 2 + half
        return pltpu.make_async_copy(
            held.at[dest % 2, page_of[dest - dest % 2 + half], :, pl.ds(0, KV_RANK)],
            out.at[dest, pl.ds(half * PAGE, PAGE)],
            lat_sem.at[index],
        )

    def ropes(dest):
        return pltpu.make_async_copy(
            packed.at[dest], out.at[dest, pl.ds(PAIR, 16)], rope_sem.at[dest]
        )

    for layer in range(2):
        fetch(layer).start()
    targets.wait()
    for page in range(PEERS):
        page_of[target_of[page]] = page
    for layer in range(2):
        fetch(layer).wait()
        for dest in range(layer, PEERS, 2):
            for half in range(2):
                latents(dest, half).start()
        for dest in range(layer, PEERS, 2):
            groups = [
                held[layer, page_of[dest - layer + half], 16 * k : 16 * k + 16, KV_RANK:]
                for half in range(2)
                for k in range(PAGE // 16)
            ]
            packed[dest] = jnp.concatenate(groups, axis=1)
            ropes(dest).start()
    for dest in range(PEERS):
        for half in range(2):
            latents(dest, half).wait()
        ropes(dest).wait()


def gather_pages(send_to, pages):
    return pl.pallas_call(
        send_kernel,
        out_shape=jax.ShapeDtypeStruct((PEERS, PAIR_ROWS, KV_RANK), jnp.bfloat16),
        in_specs=[ANY, ANY],
        out_specs=ANY,
        scratch_shapes=[
            pltpu.SMEM((PEERS,), jnp.int32),
            pltpu.SMEM((PEERS,), jnp.int32),
            pltpu.VMEM(pages.shape, jnp.bfloat16),
            pltpu.VMEM((PEERS, 16, KV_RANK), jnp.bfloat16),
            pltpu.SemaphoreType.DMA,
            pltpu.SemaphoreType.DMA((2,)),
            pltpu.SemaphoreType.DMA((2 * PEERS,)),
            pltpu.SemaphoreType.DMA((PEERS,)),
        ],
        compiler_params=pltpu.CompilerParams(vmem_limit_bytes=60 << 20),
        cost_estimate=pl.CostEstimate(flops=0, bytes_accessed=5 << 20, transcendentals=0),
    )(send_to, pages)


def around(place, step, sign):
    y = lax.rem(place // SIDE + SIDE + sign * (step // SIDE), SIDE)
    x = lax.rem(lax.rem(place, SIDE) + SIDE + sign * (step % SIDE), SIDE)
    return y * SIDE + x


def queries_kernel(where, queries, nope, rope, rows):
    rows[...] = queries[0, 0].astype(jnp.float32)
    for j in range(PEERS):
        ahead = pl.multiple_of(around(where[2], j, 1) * HEADS_PER, HEADS_PER)
        behind = pl.multiple_of(around(where[2], j, -1) * HEADS_PER, HEADS_PER)
        nope[j] = jnp.concatenate(
            [rows[t, pl.ds(ahead, HEADS_PER), :NOPE] for t in range(STEPS)], axis=0
        ).astype(jnp.bfloat16)
        rope[j * BLOCK : (j + 1) * BLOCK, :] = jnp.concatenate(
            [rows[t, pl.ds(behind, HEADS_PER), NOPE:] for t in range(STEPS)], axis=0
        ).astype(jnp.bfloat16)


def split_queries(where, queries):
    return pl.pallas_call(
        queries_kernel,
        out_shape=(
            jax.ShapeDtypeStruct((PEERS, BLOCK, NOPE), jnp.bfloat16),
            jax.ShapeDtypeStruct((ROWS, ROPE), jnp.bfloat16),
        ),
        grid_spec=pltpu.PrefetchScalarGridSpec(
            num_scalar_prefetch=1,
            grid=(1,),
            in_specs=[
                pl.BlockSpec((1,) + queries.shape[1:], lambda i, where: (where[1], 0, 0, 0, 0))
            ],
            out_specs=(
                pl.BlockSpec((PEERS, BLOCK, NOPE), lambda i, where: (0, 0, 0)),
                pl.BlockSpec((ROWS, ROPE), lambda i, where: (0, 0)),
            ),
            scratch_shapes=[pltpu.VMEM(queries.shape[2:], jnp.float32)],
        ),
        compiler_params=pltpu.CompilerParams(vmem_limit_bytes=8 << 20),
        cost_estimate=pl.CostEstimate(flops=0, bytes_accessed=600000, transcendentals=0),
    )(where, queries)


def absorb_kernel(where, heads, own, got, out):
    rows = heads[...]
    head = lax.rem(lax.broadcasted_iota(jnp.int32, rows.shape, 0), HEADS_PER)
    spread = jnp.concatenate(
        [jnp.where(head == h, rows, jnp.zeros_like(rows)) for h in range(HEADS_PER)], axis=1
    )
    for weight, half in ((own, where[1]), (got, 1 - where[1])):
        part = weight[0].reshape(HEADS_PER * NOPE, HALF)
        result = jnp.dot(spread, part, preferred_element_type=jnp.float32)
        result = result.astype(jnp.bfloat16)
        columns = pl.ds(pl.multiple_of(half * HALF, HALF), HALF)
        for j in range(PEERS):
            turned = (-(j // SIDE) % SIDE) * SIDE + -j % SIDE
            out[turned * BLOCK : (turned + 1) * BLOCK, columns] = result[j * BLOCK : (j + 1) * BLOCK]


def pick_values_kernel(where, own, got, out):
    layer = where[1]
    for weight, half in ((own, layer), (got, 1 - layer)):
        rows = pl.ds(pl.multiple_of(half * HALF, HALF), HALF)
        for h in range(HEADS_PER):
            out[h // 2, rows, h % 2 * VDIM : (h % 2 + 1) * VDIM] = weight[layer, h]


def pick_values(where, own, got):
    return pl.pallas_call(
        pick_values_kernel,
        out_shape=jax.ShapeDtypeStruct((HEADS_PER // 2, KV_RANK, 2 * VDIM), jnp.bfloat16),
        in_specs=[SMEM, VMEM, VMEM],
        out_specs=VMEM,
        compiler_params=pltpu.CompilerParams(vmem_limit_bytes=16 << 20),
        cost_estimate=pl.CostEstimate(flops=0, bytes_accessed=3 << 20, transcendentals=0),
    )(where, own, got)


def value_kernel(latent, weight, out):
    rows = latent[...]
    head = lax.rem(lax.broadcasted_iota(jnp.int32, (ROWS, VDIM), 0), HEADS_PER)
    result = jnp.zeros((ROWS, VDIM), jnp.float32)
    for p in range(HEADS_PER // 2):
        both = jnp.dot(rows, weight[p], preferred_element_type=jnp.float32)
        result = jnp.where(head == 2 * p, both[:, :VDIM], result)
        result = jnp.where(head == 2 * p + 1, both[:, VDIM:], result)
    out[...] = result.astype(jnp.bfloat16)


def project_values(latent, weight):
    return pl.pallas_call(
        value_kernel,
        out_shape=jax.ShapeDtypeStruct((ROWS, VDIM), jnp.bfloat16),
        in_specs=[VMEM, VMEM],
        out_specs=VMEM,
        compiler_params=pltpu.CompilerParams(vmem_limit_bytes=16 << 20),
        cost_estimate=pl.CostEstimate(
            flops=2 * ROWS * 1024 * KV_RANK, bytes_accessed=2 << 20, transcendentals=0
        ),
    )(latent, weight)


def project(kernel, width, where, rows, own, got):
    shape = (1,) + own.shape[1:]
    weight_spec = pl.BlockSpec(shape, lambda i, where: (where[1], 0, 0, 0))
    return pl.pallas_call(
        kernel,
        out_shape=jax.ShapeDtypeStruct((ROWS, width), jnp.bfloat16),
        grid_spec=pltpu.PrefetchScalarGridSpec(
            num_scalar_prefetch=1,
            grid=(1,),
            in_specs=[pl.BlockSpec(rows.shape, lambda i, where: (0, 0)), weight_spec, weight_spec],
            out_specs=pl.BlockSpec((ROWS, width), lambda i, where: (0, 0)),
        ),
        compiler_params=pltpu.CompilerParams(vmem_limit_bytes=24 << 20),
        cost_estimate=pl.CostEstimate(
            flops=2 * ROWS * 1024 * KV_RANK, bytes_accessed=2 << 20, transcendentals=0
        ),
    )(where, rows, own, got)


def dot_rows(a, b):
    return lax.dot_general(a, b, (((1,), (1,)), ((), ())), preferred_element_type=jnp.float32)


def attend_kernel(where, length, own_slot, other_slot, query, fresh, pages, out, ropes, scores, result, out_sem):
    layer = where[1]

    def store(j):
        return pltpu.make_async_copy(
            result.at[pl.ds(j * BLOCK, BLOCK)], out.at[around(where[2], j, -1)], out_sem.at[j]
        )

    lane = lax.broadcasted_iota(jnp.int32, (1, PAIR), 1)

    def live_of(source):
        mine, theirs = own_slot[source] * PAGE, other_slot[source] * PAGE
        first = jnp.where(layer == 0, mine, theirs)
        second = jnp.where(layer == 0, theirs, mine) + BLOCK_KEYS
        return lane < jnp.where(lane < PAGE, length[0] - first, length[0] - second + PAGE)

    for p in range(PEERS):
        for k in range(8):
            ropes[p * PAIR + 16 * k : p * PAIR + 16 * k + 16, :] = pages[
                p, PAIR:PAIR_ROWS, ROPE * k : ROPE * k + ROPE
            ]
    ql, qr = query[:, :KV_RANK], query[:, KV_RANK : KV_RANK + ROPE]
    step = lax.rem(lax.broadcasted_iota(jnp.int32, (ROWS, 16), 0) // HEADS_PER, STEPS)
    key = lax.broadcasted_iota(jnp.int32, (ROWS, 16), 1)
    lat, rope = fresh[:, :KV_RANK], fresh[:, KV_RANK:]
    extra = jnp.where(key <= step, dot_rows(ql, lat) + dot_rows(qr, rope), DEAD)
    width = 2 * PAIR
    highest = jnp.full((ROWS, PAIR), DEAD, jnp.float32)
    for n in range(0, PEERS, 2):
        part = slice(n * PAIR, n * PAIR + width)
        lat = pages[n : n + 2, :PAIR, :].reshape(width, KV_RANK)
        s = dot_rows(ql, lat) + dot_rows(qr, ropes[part, :])
        s = jnp.where(jnp.concatenate([live_of(n), live_of(n + 1)], axis=1), s, DEAD)
        scores[:, part] = s
        highest = jnp.maximum(highest, jnp.maximum(s[:, :PAIR], s[:, PAIR:]))
    peak = jnp.maximum(
        jnp.max(extra, axis=1, keepdims=True), jnp.max(highest, axis=1, keepdims=True)
    )
    weight = jnp.exp2((extra - peak) * TO_LOG2).astype(jnp.bfloat16)
    total = jnp.sum(weight.astype(jnp.float32), axis=1, keepdims=True)
    summed = jnp.dot(weight, fresh[:, :KV_RANK], preferred_element_type=jnp.float32)
    added = jnp.zeros((ROWS, PAIR), jnp.float32)
    for n in range(0, PEERS, 2):
        part = slice(n * PAIR, n * PAIR + width)
        lat = pages[n : n + 2, :PAIR, :].reshape(width, KV_RANK)
        weight = jnp.exp2((scores[:, part] - peak) * TO_LOG2).astype(jnp.bfloat16)
        kept = weight.astype(jnp.float32)
        added = added + (kept[:, :PAIR] + kept[:, PAIR:])
        summed = summed + jnp.dot(weight, lat, preferred_element_type=jnp.float32)
    total = total + jnp.sum(added, axis=1, keepdims=True)
    result[...] = (summed * (1.0 / total)).astype(jnp.bfloat16)
    for j in range(PEERS):
        store(j).start()
    for j in range(PEERS):
        store(j).wait()


def attend(*args):
    keys = PEERS * PAIR
    return pl.pallas_call(
        attend_kernel,
        out_shape=jax.ShapeDtypeStruct((PEERS, BLOCK, KV_RANK), jnp.bfloat16),
        in_specs=[SMEM] * 4 + [VMEM] * 3,
        out_specs=ANY,
        scratch_shapes=[
            pltpu.VMEM((keys, ROPE), jnp.bfloat16),
            pltpu.VMEM((ROWS, keys), jnp.float32),
            pltpu.VMEM((ROWS, KV_RANK), jnp.bfloat16),
            pltpu.SemaphoreType.DMA((PEERS,)),
        ],
        compiler_params=pltpu.CompilerParams(vmem_limit_bytes=40 << 20),
        cost_estimate=pl.CostEstimate(
            flops=2 * ROWS * keys * 1088, bytes_accessed=4 << 20, transcendentals=ROWS * keys
        ),
    )(*args)


def shifted(value, dy, dx):
    pairs = [
        (y * SIDE + x, ((y + dy) % SIDE) * SIDE + (x + dx) % SIDE)
        for y in range(SIDE)
        for x in range(SIDE)
    ]
    return lax.ppermute(value, "req", pairs)


def exchange(value):
    value = value.reshape((SIDE,) + (SIDE, BLOCK) + value.shape[1:])
    columns = [value[:, 0]] + [shifted(value[:, d], 0, d) for d in range(1, SIDE)]
    rows = jnp.stack(columns, axis=1)
    back = jnp.stack([rows[0]] + [shifted(rows[d], d, 0) for d in range(1, SIDE)])
    return back.reshape((ROWS,) + back.shape[3:])


def swapped(value):
    return lax.ppermute(value, "seq", [(0, 1), (1, 0)])


def shards(queries, w_absorb_k, w_absorb_v, prefill_pages, send_to, slot_of, lengths, new_latents):
    layer = lax.axis_index("seq")
    where = jnp.stack([lax.axis_index("group"), layer, lax.axis_index("req")]).astype(jnp.int32)

    sent = gather_pages(send_to[0, 0], prefill_pages[0, 0])
    pages = lax.all_to_all(sent, ("group", "seq"), split_axis=0, concat_axis=0, tiled=True)

    own_slot = slot_of[0, 0]
    nope, rope = split_queries(where, queries)
    heads = exchange(nope.reshape(ROWS, NOPE))
    latent = project(absorb_kernel, KV_RANK, where, heads, w_absorb_k, swapped(w_absorb_k))
    q_lat = exchange(latent)
    values = pick_values(where, w_absorb_v, swapped(w_absorb_v))

    fresh = lax.dynamic_index_in_dim(new_latents, layer, 0, keepdims=False)[0]
    fresh = jnp.pad(fresh, ((0, 16 - STEPS), (0, 0)))
    query = jnp.concatenate([q_lat, rope, jnp.zeros_like(rope)], axis=1)
    query, values = lax.optimization_barrier((query, values))
    latent_out = attend(where, lengths, own_slot, swapped(own_slot), query, fresh, pages)
    latent_heads = lax.all_to_all(latent_out, "req", split_axis=0, concat_axis=0, tiled=True)
    head_out = project_values(latent_heads.reshape(ROWS, KV_RANK), values)
    return lax.all_gather(head_out.reshape(PEERS, STEPS, HEADS_PER, VDIM), "seq", axis=0)


def solution(mesh):
    in_specs = (
        P(None, ("group", "req"), None, None, None),
        P(None, "req", None, "seq"),
        P(None, "req", "seq", None),
        P(("group", "seq"), "req", None, None, None, None),
        P(("group", "seq"), "req", None),
        P(("group", "seq"), "req", None),
        P(("group", "req")),
        P(None, ("group", "req"), None, None),
    )
    out_specs = P(None, "group", None, "req", None)
    return jax.shard_map(shards, mesh=mesh, in_specs=in_specs, out_specs=out_specs, check_vma=False)
```

```python
import functools
import math

import jax
import jax.numpy as jnp
from jax import lax
from jax.experimental import pallas as pl
from jax.experimental.pallas import tpu as pltpu
from jax.sharding import PartitionSpec as P

KV_RANK = 512
ROPE = 64
NOPE = 128
VDIM = 128
HEADS_PER = 8
STEPS = 4
PAGE = 64
PEERS = 16
BLOCK_KEYS = 1024
PAIR = 2 * PAGE
PAIR_ROWS = PAIR + 16
BLOCK = HEADS_PER * STEPS
ROWS = PEERS * BLOCK
TILE = 512
HALF = KV_RANK // 2
DEAD = -1e30
SCALE = 1.0 / math.sqrt(NOPE + ROPE)
TO_LOG2 = SCALE * math.log2(math.e)
SIDE = 4
VMEM = pl.BlockSpec(memory_space=pltpu.VMEM)
SMEM = pl.BlockSpec(memory_space=pltpu.SMEM)
ANY = pl.BlockSpec(memory_space=pl.ANY)


def send_kernel(send_to, pages, out, target_of, page_of, held, packed, target_sem, in_sem, lat_sem, rope_sem):
    targets = pltpu.make_async_copy(send_to, target_of, target_sem)
    targets.start()

    def fetch(layer):
        return pltpu.make_async_copy(pages.at[layer], held.at[layer], in_sem.at[layer])

    def latents(dest, half):
        index = dest * 2 + half
        return pltpu.make_async_copy(
            held.at[dest % 2, page_of[dest - dest % 2 + half], :, pl.ds(0, KV_RANK)],
            out.at[dest, pl.ds(half * PAGE, PAGE)],
            lat_sem.at[index],
        )

    def ropes(dest):
        return pltpu.make_async_copy(
            packed.at[dest], out.at[dest, pl.ds(PAIR, 16)], rope_sem.at[dest]
        )

    for layer in range(2):
        fetch(layer).start()
    targets.wait()
    for page in range(PEERS):
        page_of[target_of[page]] = page
    for layer in range(2):
        fetch(layer).wait()
        for dest in range(layer, PEERS, 2):
            for half in range(2):
                latents(dest, half).start()
        for dest in range(layer, PEERS, 2):
            groups = [
                held[layer, page_of[dest - layer + half], 16 * k : 16 * k + 16, KV_RANK:]
                for half in range(2)
                for k in range(PAGE // 16)
            ]
            packed[dest] = jnp.concatenate(groups, axis=1)
            ropes(dest).start()
    for dest in range(PEERS):
        for half in range(2):
            latents(dest, half).wait()
        ropes(dest).wait()


def gather_pages(send_to, pages):
    return pl.pallas_call(
        send_kernel,
        out_shape=jax.ShapeDtypeStruct((PEERS, PAIR_ROWS, KV_RANK), jnp.bfloat16),
        in_specs=[ANY, ANY],
        out_specs=ANY,
        scratch_shapes=[
            pltpu.SMEM((PEERS,), jnp.int32),
            pltpu.SMEM((PEERS,), jnp.int32),
            pltpu.VMEM(pages.shape, jnp.bfloat16),
            pltpu.VMEM((PEERS, 16, KV_RANK), jnp.bfloat16),
            pltpu.SemaphoreType.DMA,
            pltpu.SemaphoreType.DMA((2,)),
            pltpu.SemaphoreType.DMA((2 * PEERS,)),
            pltpu.SemaphoreType.DMA((PEERS,)),
        ],
        compiler_params=pltpu.CompilerParams(vmem_limit_bytes=60 << 20),
        cost_estimate=pl.CostEstimate(flops=0, bytes_accessed=5 << 20, transcendentals=0),
    )(send_to, pages)


def around(place, step, sign):
    y = lax.rem(place // SIDE + SIDE + sign * (step // SIDE), SIDE)
    x = lax.rem(lax.rem(place, SIDE) + SIDE + sign * (step % SIDE), SIDE)
    return y * SIDE + x


def queries_kernel(where, queries, nope, rope, rows):
    rows[...] = queries[0, 0].astype(jnp.float32)
    for j in range(PEERS):
        ahead = pl.multiple_of(around(where[2], j, 1) * HEADS_PER, HEADS_PER)
        behind = pl.multiple_of(around(where[2], j, -1) * HEADS_PER, HEADS_PER)
        nope[j] = jnp.concatenate(
            [rows[t, pl.ds(ahead, HEADS_PER), :NOPE] for t in range(STEPS)], axis=0
        ).astype(jnp.bfloat16)
        rope[j * BLOCK : (j + 1) * BLOCK, :] = jnp.concatenate(
            [rows[t, pl.ds(behind, HEADS_PER), NOPE:] for t in range(STEPS)], axis=0
        ).astype(jnp.bfloat16)


def split_queries(where, queries):
    return pl.pallas_call(
        queries_kernel,
        out_shape=(
            jax.ShapeDtypeStruct((PEERS, BLOCK, NOPE), jnp.bfloat16),
            jax.ShapeDtypeStruct((ROWS, ROPE), jnp.bfloat16),
        ),
        grid_spec=pltpu.PrefetchScalarGridSpec(
            num_scalar_prefetch=1,
            grid=(1,),
            in_specs=[
                pl.BlockSpec((1,) + queries.shape[1:], lambda i, where: (where[1], 0, 0, 0, 0))
            ],
            out_specs=(
                pl.BlockSpec((PEERS, BLOCK, NOPE), lambda i, where: (0, 0, 0)),
                pl.BlockSpec((ROWS, ROPE), lambda i, where: (0, 0)),
            ),
            scratch_shapes=[pltpu.VMEM(queries.shape[2:], jnp.float32)],
        ),
        compiler_params=pltpu.CompilerParams(vmem_limit_bytes=8 << 20),
        cost_estimate=pl.CostEstimate(flops=0, bytes_accessed=600000, transcendentals=0),
    )(where, queries)


def absorb_kernel(where, heads, own, got, out):
    rows = heads[...]
    head = lax.rem(lax.broadcasted_iota(jnp.int32, rows.shape, 0), HEADS_PER)
    spread = jnp.concatenate(
        [jnp.where(head == h, rows, jnp.zeros_like(rows)) for h in range(HEADS_PER)], axis=1
    )
    for weight, half in ((own, where[1]), (got, 1 - where[1])):
        part = weight[0].reshape(HEADS_PER * NOPE, HALF)
        result = jnp.dot(spread, part, preferred_element_type=jnp.float32)
        result = result.astype(jnp.bfloat16)
        columns = pl.ds(pl.multiple_of(half * HALF, HALF), HALF)
        for j in range(PEERS):
            turned = (-(j // SIDE) % SIDE) * SIDE + -j % SIDE
            out[turned * BLOCK : (turned + 1) * BLOCK, columns] = result[j * BLOCK : (j + 1) * BLOCK]


def pick_values_kernel(where, own, got, out):
    layer = where[1]
    for weight, half in ((own, layer), (got, 1 - layer)):
        rows = pl.ds(pl.multiple_of(half * HALF, HALF), HALF)
        for h in range(HEADS_PER):
            out[h // 2, rows, h % 2 * VDIM : (h % 2 + 1) * VDIM] = weight[layer, h]


def pick_values(where, own, got):
    return pl.pallas_call(
        pick_values_kernel,
        out_shape=jax.ShapeDtypeStruct((HEADS_PER // 2 + 1, KV_RANK, 2 * VDIM), jnp.bfloat16),
        in_specs=[SMEM, VMEM, VMEM],
        out_specs=VMEM,
        compiler_params=pltpu.CompilerParams(vmem_limit_bytes=16 << 20),
        cost_estimate=pl.CostEstimate(flops=0, bytes_accessed=3 << 20, transcendentals=0),
    )(where, own, got)


def value_kernel(latent, weight, out):
    rows = latent[...]
    head = lax.rem(lax.broadcasted_iota(jnp.int32, (ROWS, VDIM), 0), HEADS_PER)
    result = jnp.zeros((ROWS, VDIM), jnp.float32)
    for p in range(HEADS_PER // 2):
        both = jnp.dot(rows, weight[p], preferred_element_type=jnp.float32)
        result = jnp.where(head == 2 * p, both[:, :VDIM], result)
        result = jnp.where(head == 2 * p + 1, both[:, VDIM:], result)
    out[...] = result.astype(jnp.bfloat16)


def project_values(latent, weight):
    return pl.pallas_call(
        value_kernel,
        out_shape=jax.ShapeDtypeStruct((ROWS, VDIM), jnp.bfloat16),
        in_specs=[VMEM, VMEM],
        out_specs=VMEM,
        compiler_params=pltpu.CompilerParams(vmem_limit_bytes=16 << 20),
        cost_estimate=pl.CostEstimate(
            flops=2 * ROWS * 1024 * KV_RANK, bytes_accessed=2 << 20, transcendentals=0
        ),
    )(latent, weight)


def project(kernel, width, where, rows, own, got):
    shape = (1,) + own.shape[1:]
    weight_spec = pl.BlockSpec(shape, lambda i, where: (where[1], 0, 0, 0))
    return pl.pallas_call(
        kernel,
        out_shape=jax.ShapeDtypeStruct((ROWS, width), jnp.bfloat16),
        grid_spec=pltpu.PrefetchScalarGridSpec(
            num_scalar_prefetch=1,
            grid=(1,),
            in_specs=[pl.BlockSpec(rows.shape, lambda i, where: (0, 0)), weight_spec, weight_spec],
            out_specs=pl.BlockSpec((ROWS, width), lambda i, where: (0, 0)),
        ),
        compiler_params=pltpu.CompilerParams(vmem_limit_bytes=24 << 20),
        cost_estimate=pl.CostEstimate(
            flops=2 * ROWS * 1024 * KV_RANK, bytes_accessed=2 << 20, transcendentals=0
        ),
    )(where, rows, own, got)


def dot_rows(a, b):
    return lax.dot_general(a, b, (((1,), (1,)), ((), ())), preferred_element_type=jnp.float32)


def attend_kernel(where, inputs, pages, out, ropes, scores):
    for p in range(PEERS):
        for k in range(8):
            ropes[p * PAIR + 16 * k : p * PAIR + 16 * k + 16, :] = pages[
                p, PAIR:PAIR_ROWS, ROPE * k : ROPE * k + ROPE
            ]
    width = 2 * PAIR
    fresh = inputs[ROWS : ROWS + 16, :KV_RANK]
    fresh_rope = inputs[ROWS : ROWS + 16, KV_RANK : KV_RANK + ROPE]
    live = inputs[ROWS + 16 :, :PAIR].astype(jnp.float32) > 0.5

    def tile(first):
        rows = pl.ds(first, TILE)
        ql, qr = inputs[rows, :KV_RANK], inputs[rows, KV_RANK : KV_RANK + ROPE]
        row = lax.broadcasted_iota(jnp.int32, (TILE, 16), 0)
        key = lax.broadcasted_iota(jnp.int32, (TILE, 16), 1)
        extra = dot_rows(ql, fresh) + dot_rows(qr, fresh_rope)
        extra = jnp.where(key <= lax.rem(row // HEADS_PER, STEPS), extra, DEAD)
        highest = jnp.full((TILE, PAIR), DEAD, jnp.float32)
        for n in range(0, PEERS, 2):
            part = slice(n * PAIR, n * PAIR + width)
            lat = pages[n : n + 2, :PAIR, :].reshape(width, KV_RANK)
            s = dot_rows(ql, lat) + dot_rows(qr, ropes[part, :])
            bound = jnp.concatenate([live[n : n + 1], live[n + 1 : n + 2]], axis=1)
            s = jnp.where(bound, s, DEAD)
            scores[:, part] = s
            highest = jnp.maximum(highest, jnp.maximum(s[:, :PAIR], s[:, PAIR:]))
        peak = jnp.maximum(
            jnp.max(extra, axis=1, keepdims=True), jnp.max(highest, axis=1, keepdims=True)
        )
        weight = jnp.exp2((extra - peak) * TO_LOG2).astype(jnp.bfloat16)
        total = jnp.sum(weight.astype(jnp.float32), axis=1, keepdims=True)
        summed = jnp.dot(weight, fresh, preferred_element_type=jnp.float32)
        added = jnp.zeros((TILE, PAIR), jnp.float32)
        for n in range(0, PEERS, 2):
            part = slice(n * PAIR, n * PAIR + width)
            lat = pages[n : n + 2, :PAIR, :].reshape(width, KV_RANK)
            weight = jnp.exp2((scores[:, part] - peak) * TO_LOG2).astype(jnp.bfloat16)
            kept = weight.astype(jnp.float32)
            added = added + (kept[:, :PAIR] + kept[:, PAIR:])
            summed = summed + jnp.dot(weight, lat, preferred_element_type=jnp.float32)
        total = total + jnp.sum(added, axis=1, keepdims=True)
        result = (summed * (1.0 / total)).astype(jnp.bfloat16)
        for k in range(TILE // BLOCK):
            j = around(where[2], first // BLOCK + k, -1)
            out[j] = result[k * BLOCK : (k + 1) * BLOCK]

    for first in range(0, ROWS, TILE):
        tile(first)


def attend(where, inputs, pages):
    keys = PEERS * PAIR
    return pl.pallas_call(
        attend_kernel,
        out_shape=jax.ShapeDtypeStruct((PEERS, BLOCK, KV_RANK), jnp.bfloat16),
        in_specs=[SMEM, VMEM, VMEM],
        out_specs=VMEM,
        scratch_shapes=[
            pltpu.VMEM((keys, ROPE), jnp.bfloat16),
            pltpu.VMEM((TILE, keys), jnp.float32),
        ],
        compiler_params=pltpu.CompilerParams(vmem_limit_bytes=40 << 20),
        cost_estimate=pl.CostEstimate(
            flops=2 * ROWS * keys * 1088, bytes_accessed=4 << 20, transcendentals=ROWS * keys
        ),
    )(where, inputs, pages)


def shifted(value, dy, dx):
    pairs = [
        (y * SIDE + x, ((y + dy) % SIDE) * SIDE + (x + dx) % SIDE)
        for y in range(SIDE)
        for x in range(SIDE)
    ]
    return lax.ppermute(value, "req", pairs)


def exchange(value):
    value = value.reshape((SIDE,) + (SIDE, BLOCK) + value.shape[1:])
    columns = [value[:, 0]] + [shifted(value[:, d], 0, d) for d in range(1, SIDE)]
    rows = jnp.stack(columns, axis=1)
    back = jnp.stack([rows[0]] + [shifted(rows[d], d, 0) for d in range(1, SIDE)])
    return back.reshape((ROWS,) + back.shape[3:])


def swapped(value):
    return lax.ppermute(value, "seq", [(0, 1), (1, 0)])


def shards(queries, w_absorb_k, w_absorb_v, prefill_pages, send_to, slot_of, lengths, new_latents):
    layer = lax.axis_index("seq")
    where = jnp.stack([lax.axis_index("group"), layer, lax.axis_index("req")]).astype(jnp.int32)

    sent = gather_pages(send_to[0, 0], prefill_pages[0, 0])
    pages = lax.all_to_all(sent, ("group", "seq"), split_axis=0, concat_axis=0, tiled=True)

    own_slot = slot_of[0, 0]
    nope, rope = split_queries(where, queries)
    heads = exchange(nope.reshape(ROWS, NOPE))
    latent = project(absorb_kernel, KV_RANK, where, heads, w_absorb_k, swapped(w_absorb_k))
    q_lat = exchange(latent)
    values = pick_values(where, w_absorb_v, swapped(w_absorb_v))

    fresh = lax.dynamic_index_in_dim(new_latents, layer, 0, keepdims=False)[0]
    slots = jnp.stack([own_slot, swapped(own_slot)])
    slots = jnp.where(layer == 0, slots, slots[::-1])
    starts = slots.T * PAGE + jnp.arange(2, dtype=jnp.int32) * BLOCK_KEYS
    live = starts[:, :, None] + jnp.arange(PAGE, dtype=jnp.int32) < lengths[0]
    inputs = jnp.concatenate(
        [
            jnp.concatenate([q_lat, rope, jnp.zeros_like(rope)], axis=1),
            jnp.pad(fresh, ((0, 16 - STEPS), (0, ROPE))),
            jnp.pad(live.reshape(PEERS, PAIR).astype(jnp.bfloat16), ((0, 0), (0, KV_RANK))),
        ]
    )
    inputs, values = lax.optimization_barrier((inputs, values))
    latent_out = attend(where, inputs, pages)
    latent_heads = lax.all_to_all(latent_out, "req", split_axis=0, concat_axis=0, tiled=True)
    head_out = project_values(latent_heads.reshape(ROWS, KV_RANK), values)
    return lax.all_gather(head_out.reshape(PEERS, STEPS, HEADS_PER, VDIM), "seq", axis=0)


def solution(mesh):
    in_specs = (
        P(None, ("group", "req"), None, None, None),
        P(None, "req", None, "seq"),
        P(None, "req", "seq", None),
        P(("group", "seq"), "req", None, None, None, None),
        P(("group", "seq"), "req", None),
        P(("group", "seq"), "req", None),
        P(("group", "req")),
        P(None, ("group", "req"), None, None),
    )
    out_specs = P(None, "group", None, "req", None)
    return jax.shard_map(shards, mesh=mesh, in_specs=in_specs, out_specs=out_specs, check_vma=False)
```

```python
import functools
import math

import jax
import jax.numpy as jnp
from jax import lax
from jax.experimental import pallas as pl
from jax.experimental.pallas import tpu as pltpu
from jax.sharding import PartitionSpec as P

KV_RANK = 512
ROPE = 64
NOPE = 128
VDIM = 128
HEADS_PER = 8
STEPS = 4
PAGE = 64
PEERS = 16
BLOCK_KEYS = 1024
PAIR = 2 * PAGE
PAIR_ROWS = PAIR + 16
BLOCK = HEADS_PER * STEPS
ROWS = PEERS * BLOCK
TILE = 512
CHUNK = 2
HALF = KV_RANK // 2
DEAD = -1e30
SCALE = 1.0 / math.sqrt(NOPE + ROPE)
TO_LOG2 = SCALE * math.log2(math.e)
SIDE = 4
VMEM = pl.BlockSpec(memory_space=pltpu.VMEM)
SMEM = pl.BlockSpec(memory_space=pltpu.SMEM)
ANY = pl.BlockSpec(memory_space=pl.ANY)


def send_kernel(send_to, pages, out, target_of, held, packed, target_sem, in_sem, lat_sem, rope_sem):
    targets = pltpu.make_async_copy(send_to, target_of, target_sem)
    targets.start()

    def fetch(part):
        some = pl.ds(part * CHUNK, CHUNK)
        return pltpu.make_async_copy(pages.at[:, some], held.at[:, some], in_sem.at[part])

    def latents(layer, page):
        target = target_of[page]
        return pltpu.make_async_copy(
            held.at[layer, page, :, pl.ds(0, KV_RANK)],
            out.at[target // 2 * 2 + layer, pl.ds(target % 2 * PAGE, PAGE)],
            lat_sem.at[layer, page],
        )

    for part in range(PEERS // CHUNK):
        fetch(part).start()
    targets.wait()
    for part in range(PEERS // CHUNK):
        fetch(part).wait()
        for page in range(part * CHUNK, (part + 1) * CHUNK):
            for layer in range(2):
                latents(layer, page).start()
        for page in range(part * CHUNK, (part + 1) * CHUNK):
            target = target_of[page]
            columns = pl.ds(pl.multiple_of(target % 2 * (KV_RANK // 2), KV_RANK // 2), KV_RANK // 2)
            for layer in range(2):
                packed[target // 2 * 2 + layer, :, columns] = jnp.concatenate(
                    [held[layer, page, 16 * k : 16 * k + 16, KV_RANK:] for k in range(PAGE // 16)],
                    axis=1,
                )
    ropes = pltpu.make_async_copy(packed, out.at[:, pl.ds(PAIR, 16)], rope_sem)
    ropes.start()
    for page in range(PEERS):
        for layer in range(2):
            latents(layer, page).wait()
    ropes.wait()


def gather_pages(send_to, pages):
    return pl.pallas_call(
        send_kernel,
        out_shape=jax.ShapeDtypeStruct((PEERS, PAIR_ROWS, KV_RANK), jnp.bfloat16),
        in_specs=[ANY, ANY],
        out_specs=ANY,
        scratch_shapes=[
            pltpu.SMEM((PEERS,), jnp.int32),
            pltpu.VMEM(pages.shape, jnp.bfloat16),
            pltpu.VMEM((PEERS, 16, KV_RANK), jnp.bfloat16),
            pltpu.SemaphoreType.DMA,
            pltpu.SemaphoreType.DMA((PEERS // CHUNK,)),
            pltpu.SemaphoreType.DMA((2, PEERS)),
            pltpu.SemaphoreType.DMA,
        ],
        compiler_params=pltpu.CompilerParams(vmem_limit_bytes=60 << 20),
        cost_estimate=pl.CostEstimate(flops=0, bytes_accessed=5 << 20, transcendentals=0),
    )(send_to, pages)


def around(place, step, sign):
    y = lax.rem(place // SIDE + SIDE + sign * (step // SIDE), SIDE)
    x = lax.rem(lax.rem(place, SIDE) + SIDE + sign * (step % SIDE), SIDE)
    return y * SIDE + x


def queries_kernel(where, queries, nope, rope, rows):
    rows[...] = queries[0, 0].astype(jnp.float32)
    for j in range(PEERS):
        ahead = pl.multiple_of(around(where[2], j, 1) * HEADS_PER, HEADS_PER)
        behind = pl.multiple_of(around(where[2], j, -1) * HEADS_PER, HEADS_PER)
        nope[j] = jnp.concatenate(
            [rows[t, pl.ds(ahead, HEADS_PER), :NOPE] for t in range(STEPS)], axis=0
        ).astype(jnp.bfloat16)
        rope[j * BLOCK : (j + 1) * BLOCK, :] = jnp.concatenate(
            [rows[t, pl.ds(behind, HEADS_PER), NOPE:] for t in range(STEPS)], axis=0
        ).astype(jnp.bfloat16)


def split_queries(where, queries):
    return pl.pallas_call(
        queries_kernel,
        out_shape=(
            jax.ShapeDtypeStruct((PEERS, BLOCK, NOPE), jnp.bfloat16),
            jax.ShapeDtypeStruct((ROWS, ROPE), jnp.bfloat16),
        ),
        grid_spec=pltpu.PrefetchScalarGridSpec(
            num_scalar_prefetch=1,
            grid=(1,),
            in_specs=[
                pl.BlockSpec((1,) + queries.shape[1:], lambda i, where: (where[1], 0, 0, 0, 0))
            ],
            out_specs=(
                pl.BlockSpec((PEERS, BLOCK, NOPE), lambda i, where: (0, 0, 0)),
                pl.BlockSpec((ROWS, ROPE), lambda i, where: (0, 0)),
            ),
            scratch_shapes=[pltpu.VMEM(queries.shape[2:], jnp.float32)],
        ),
        compiler_params=pltpu.CompilerParams(vmem_limit_bytes=8 << 20),
        cost_estimate=pl.CostEstimate(flops=0, bytes_accessed=600000, transcendentals=0),
    )(where, queries)


def absorb_kernel(where, heads, own, got, out):
    rows = heads[...]
    head = lax.rem(lax.broadcasted_iota(jnp.int32, rows.shape, 0), HEADS_PER)
    spread = jnp.concatenate(
        [jnp.where(head == h, rows, jnp.zeros_like(rows)) for h in range(HEADS_PER)], axis=1
    )
    for weight, half in ((own, where[1]), (got, 1 - where[1])):
        part = weight[0].reshape(HEADS_PER * NOPE, HALF)
        result = jnp.dot(spread, part, preferred_element_type=jnp.float32)
        result = result.astype(jnp.bfloat16)
        columns = pl.ds(pl.multiple_of(half * HALF, HALF), HALF)
        for j in range(PEERS):
            turned = (-(j // SIDE) % SIDE) * SIDE + -j % SIDE
            out[turned * BLOCK : (turned + 1) * BLOCK, columns] = result[j * BLOCK : (j + 1) * BLOCK]


def pick_values_kernel(where, own, got, out):
    layer = where[1]
    for weight, half in ((own, layer), (got, 1 - layer)):
        rows = pl.ds(pl.multiple_of(half * HALF, HALF), HALF)
        for h in range(HEADS_PER):
            out[h // 2, rows, h % 2 * VDIM : (h % 2 + 1) * VDIM] = weight[layer, h]


def pick_values(where, own, got):
    return pl.pallas_call(
        pick_values_kernel,
        out_shape=jax.ShapeDtypeStruct((HEADS_PER // 2 + 1, KV_RANK, 2 * VDIM), jnp.bfloat16),
        in_specs=[SMEM, VMEM, VMEM],
        out_specs=VMEM,
        compiler_params=pltpu.CompilerParams(vmem_limit_bytes=16 << 20),
        cost_estimate=pl.CostEstimate(flops=0, bytes_accessed=3 << 20, transcendentals=0),
    )(where, own, got)


def value_kernel(latent, weight, out):
    rows = latent[...]
    head = lax.rem(lax.broadcasted_iota(jnp.int32, (ROWS, VDIM), 0), HEADS_PER)
    result = jnp.zeros((ROWS, VDIM), jnp.float32)
    for p in range(HEADS_PER // 2):
        both = jnp.dot(rows, weight[p], preferred_element_type=jnp.float32)
        result = jnp.where(head == 2 * p, both[:, :VDIM], result)
        result = jnp.where(head == 2 * p + 1, both[:, VDIM:], result)
    out[...] = result.astype(jnp.bfloat16)


def project_values(latent, weight):
    return pl.pallas_call(
        value_kernel,
        out_shape=jax.ShapeDtypeStruct((ROWS, VDIM), jnp.bfloat16),
        in_specs=[VMEM, VMEM],
        out_specs=VMEM,
        compiler_params=pltpu.CompilerParams(vmem_limit_bytes=16 << 20),
        cost_estimate=pl.CostEstimate(
            flops=2 * ROWS * 1024 * KV_RANK, bytes_accessed=2 << 20, transcendentals=0
        ),
    )(latent, weight)


def project(kernel, width, where, rows, own, got):
    shape = (1,) + own.shape[1:]
    weight_spec = pl.BlockSpec(shape, lambda i, where: (where[1], 0, 0, 0))
    return pl.pallas_call(
        kernel,
        out_shape=jax.ShapeDtypeStruct((ROWS, width), jnp.bfloat16),
        grid_spec=pltpu.PrefetchScalarGridSpec(
            num_scalar_prefetch=1,
            grid=(1,),
            in_specs=[pl.BlockSpec(rows.shape, lambda i, where: (0, 0)), weight_spec, weight_spec],
            out_specs=pl.BlockSpec((ROWS, width), lambda i, where: (0, 0)),
        ),
        compiler_params=pltpu.CompilerParams(vmem_limit_bytes=24 << 20),
        cost_estimate=pl.CostEstimate(
            flops=2 * ROWS * 1024 * KV_RANK, bytes_accessed=2 << 20, transcendentals=0
        ),
    )(where, rows, own, got)


def dot_rows(a, b):
    return lax.dot_general(a, b, (((1,), (1,)), ((), ())), preferred_element_type=jnp.float32)


def attend_kernel(where, inputs, pages, out, ropes, scores):
    for p in range(PEERS):
        for k in range(8):
            ropes[p * PAIR + 16 * k : p * PAIR + 16 * k + 16, :] = pages[
                p, PAIR:PAIR_ROWS, ROPE * k : ROPE * k + ROPE
            ]
    width = 4 * PAIR
    fresh = inputs[ROWS : ROWS + 16, :KV_RANK]
    fresh_rope = inputs[ROWS : ROWS + 16, KV_RANK : KV_RANK + ROPE]
    live = inputs[ROWS + 16 :, :PAIR].astype(jnp.float32) > 0.5

    def tile(first):
        rows = pl.ds(first, TILE)
        ql, qr = inputs[rows, :KV_RANK], inputs[rows, KV_RANK : KV_RANK + ROPE]
        row = lax.broadcasted_iota(jnp.int32, (TILE, 16), 0)
        key = lax.broadcasted_iota(jnp.int32, (TILE, 16), 1)
        extra = dot_rows(ql, fresh) + dot_rows(qr, fresh_rope)
        extra = jnp.where(key <= lax.rem(row // HEADS_PER, STEPS), extra, DEAD)
        highest = jnp.full((TILE, PAIR), DEAD, jnp.float32)
        for n in range(0, PEERS, 4):
            part = slice(n * PAIR, n * PAIR + width)
            lat = pages[n : n + 4, :PAIR, :].reshape(width, KV_RANK)
            s = dot_rows(ql, lat) + dot_rows(qr, ropes[part, :])
            bound = jnp.concatenate([live[p : p + 1] for p in range(n, n + 4)], axis=1)
            s = jnp.where(bound, s, DEAD)
            scores[:, part] = s
            for k in range(0, width, PAIR):
                highest = jnp.maximum(highest, s[:, k : k + PAIR])
        peak = jnp.maximum(
            jnp.max(extra, axis=1, keepdims=True), jnp.max(highest, axis=1, keepdims=True)
        )
        weight = jnp.exp2((extra - peak) * TO_LOG2).astype(jnp.bfloat16)
        total = jnp.sum(weight.astype(jnp.float32), axis=1, keepdims=True)
        summed = jnp.dot(weight, fresh, preferred_element_type=jnp.float32)
        added = jnp.zeros((TILE, PAIR), jnp.float32)
        for n in range(0, PEERS, 4):
            part = slice(n * PAIR, n * PAIR + width)
            lat = pages[n : n + 4, :PAIR, :].reshape(width, KV_RANK)
            weight = jnp.exp2((scores[:, part] - peak) * TO_LOG2).astype(jnp.bfloat16)
            kept = weight.astype(jnp.float32)
            for k in range(0, width, PAIR):
                added = added + kept[:, k : k + PAIR]
            summed = summed + jnp.dot(weight, lat, preferred_element_type=jnp.float32)
        total = total + jnp.sum(added, axis=1, keepdims=True)
        result = (summed * (1.0 / total)).astype(jnp.bfloat16)
        for k in range(TILE // BLOCK):
            j = around(where[2], first // BLOCK + k, -1)
            out[j] = result[k * BLOCK : (k + 1) * BLOCK]

    for first in range(0, ROWS, TILE):
        tile(first)


def attend(where, inputs, pages):
    keys = PEERS * PAIR
    return pl.pallas_call(
        attend_kernel,
        out_shape=jax.ShapeDtypeStruct((PEERS, BLOCK, KV_RANK), jnp.bfloat16),
        in_specs=[SMEM, VMEM, VMEM],
        out_specs=VMEM,
        scratch_shapes=[
            pltpu.VMEM((keys, ROPE), jnp.bfloat16),
            pltpu.VMEM((TILE, keys), jnp.float32),
        ],
        compiler_params=pltpu.CompilerParams(vmem_limit_bytes=40 << 20),
        cost_estimate=pl.CostEstimate(
            flops=2 * ROWS * keys * 1088, bytes_accessed=4 << 20, transcendentals=ROWS * keys
        ),
    )(where, inputs, pages)


def shifted(value, dy, dx):
    pairs = [
        (y * SIDE + x, ((y + dy) % SIDE) * SIDE + (x + dx) % SIDE)
        for y in range(SIDE)
        for x in range(SIDE)
    ]
    return lax.ppermute(value, "req", pairs)


def exchange(value):
    value = value.reshape((SIDE,) + (SIDE, BLOCK) + value.shape[1:])
    columns = [value[:, 0]] + [shifted(value[:, d], 0, d) for d in range(1, SIDE)]
    rows = jnp.stack(columns, axis=1)
    back = jnp.stack([rows[0]] + [shifted(rows[d], d, 0) for d in range(1, SIDE)])
    return back.reshape((ROWS,) + back.shape[3:])


def swapped(value):
    return lax.ppermute(value, "seq", [(0, 1), (1, 0)])


def shards(queries, w_absorb_k, w_absorb_v, prefill_pages, send_to, slot_of, lengths, new_latents):
    layer = lax.axis_index("seq")
    where = jnp.stack([lax.axis_index("group"), layer, lax.axis_index("req")]).astype(jnp.int32)

    sent = gather_pages(send_to[0, 0], prefill_pages[0, 0])
    pages = lax.all_to_all(sent, ("group", "seq"), split_axis=0, concat_axis=0, tiled=True)

    own_slot = slot_of[0, 0]
    nope, rope = split_queries(where, queries)
    heads = exchange(nope.reshape(ROWS, NOPE))
    latent = project(absorb_kernel, KV_RANK, where, heads, w_absorb_k, swapped(w_absorb_k))
    q_lat = exchange(latent)
    values = pick_values(where, w_absorb_v, swapped(w_absorb_v))

    fresh = lax.dynamic_index_in_dim(new_latents, layer, 0, keepdims=False)[0]
    slots = jnp.stack([own_slot, swapped(own_slot)])
    slots = jnp.where(layer == 0, slots, slots[::-1])
    starts = slots.T * PAGE + jnp.arange(2, dtype=jnp.int32) * BLOCK_KEYS
    live = starts[:, :, None] + jnp.arange(PAGE, dtype=jnp.int32) < lengths[0]
    inputs = jnp.concatenate(
        [
            jnp.concatenate([q_lat, rope, jnp.zeros_like(rope)], axis=1),
            jnp.pad(fresh, ((0, 16 - STEPS), (0, ROPE))),
            jnp.pad(live.reshape(PEERS, PAIR).astype(jnp.bfloat16), ((0, 0), (0, KV_RANK))),
        ]
    )
    inputs, values = lax.optimization_barrier((inputs, values))
    latent_out = attend(where, inputs, pages)
    latent_heads = lax.all_to_all(latent_out, "req", split_axis=0, concat_axis=0, tiled=True)
    head_out = project_values(latent_heads.reshape(ROWS, KV_RANK), values)
    own = head_out.reshape(PEERS, STEPS, HEADS_PER, VDIM)
    got = swapped(own)
    return jnp.where(layer == 0, jnp.stack([own, got]), jnp.stack([got, own]))


def solution(mesh):
    in_specs = (
        P(None, ("group", "req"), None, None, None),
        P(None, "req", None, "seq"),
        P(None, "req", "seq", None),
        P(("group", "seq"), "req", None, None, None, None),
        P(("group", "seq"), "req", None),
        P(("group", "seq"), "req", None),
        P(("group", "req")),
        P(None, ("group", "req"), None, None),
    )
    out_specs = P(None, "group", None, "req", None)
    return jax.shard_map(shards, mesh=mesh, in_specs=in_specs, out_specs=out_specs, check_vma=False)
```

```python
import functools
import math

import jax
import jax.numpy as jnp
import numpy as np
from jax import lax
from jax.experimental import pallas as pl
from jax.experimental.pallas import tpu as pltpu
from jax.sharding import PartitionSpec as P

KV_RANK = 512
ROPE = 64
NOPE = 128
VDIM = 128
HEADS_PER = 8
STEPS = 4
PAGE = 64
PEERS = 16
BLOCK_KEYS = 1024
PAIR = 2 * PAGE
PAIR_ROWS = PAIR + 16
BLOCK = HEADS_PER * STEPS
ROWS = PEERS * BLOCK
TILE = 512
CHUNK = 2
COLUMN = (12, 15, 2, 1, 8, 0, 13, 6, 9, 3, 7, 4, 11, 10, 14, 5)
PLANE = (2, 11, 3, 10, 0, 4, 7, 5, 14, 12, 6, 9, 13, 8, 1, 15)
HALF = KV_RANK // 2
DEAD = -1e30
SCALE = 1.0 / math.sqrt(NOPE + ROPE)
TO_LOG2 = SCALE * math.log2(math.e)
SIDE = 4
VMEM = pl.BlockSpec(memory_space=pltpu.VMEM)
SMEM = pl.BlockSpec(memory_space=pltpu.SMEM)
ANY = pl.BlockSpec(memory_space=pl.ANY)


def send_kernel(send_to, order, pages, out, target_of, rank_of, held, packed, target_sem, in_sem, lat_sem, rope_sem):
    targets = pltpu.make_async_copy(send_to, target_of, target_sem.at[0])
    ranks = pltpu.make_async_copy(order, rank_of, target_sem.at[1])
    targets.start()
    ranks.start()

    def fetch(part):
        some = pl.ds(part * CHUNK, CHUNK)
        return pltpu.make_async_copy(pages.at[:, some], held.at[:, some], in_sem.at[part])

    def latents(layer, page):
        target = target_of[page]
        return pltpu.make_async_copy(
            held.at[layer, page, :, pl.ds(0, KV_RANK)],
            out.at[rank_of[target // 2 * 2 + layer], pl.ds(target % 2 * PAGE, PAGE)],
            lat_sem.at[layer, page],
        )

    for part in range(PEERS // CHUNK):
        fetch(part).start()
    targets.wait()
    ranks.wait()
    for part in range(PEERS // CHUNK):
        fetch(part).wait()
        for page in range(part * CHUNK, (part + 1) * CHUNK):
            for layer in range(2):
                latents(layer, page).start()
        for page in range(part * CHUNK, (part + 1) * CHUNK):
            target = target_of[page]
            columns = pl.ds(pl.multiple_of(target % 2 * (KV_RANK // 2), KV_RANK // 2), KV_RANK // 2)
            for layer in range(2):
                packed[rank_of[target // 2 * 2 + layer], :, columns] = jnp.concatenate(
                    [held[layer, page, 16 * k : 16 * k + 16, KV_RANK:] for k in range(PAGE // 16)],
                    axis=1,
                )
    ropes = pltpu.make_async_copy(packed, out.at[:, pl.ds(PAIR, 16)], rope_sem)
    ropes.start()
    for page in range(PEERS):
        for layer in range(2):
            latents(layer, page).wait()
    ropes.wait()


def gather_pages(send_to, pages):
    return pl.pallas_call(
        send_kernel,
        out_shape=jax.ShapeDtypeStruct((PEERS, PAIR_ROWS, KV_RANK), jnp.bfloat16),
        in_specs=[ANY, ANY, ANY],
        out_specs=ANY,
        scratch_shapes=[
            pltpu.SMEM((PEERS,), jnp.int32),
            pltpu.SMEM((PEERS,), jnp.int32),
            pltpu.VMEM(pages.shape, jnp.bfloat16),
            pltpu.VMEM((PEERS, 16, KV_RANK), jnp.bfloat16),
            pltpu.SemaphoreType.DMA((2,)),
            pltpu.SemaphoreType.DMA((PEERS // CHUNK,)),
            pltpu.SemaphoreType.DMA((2, PEERS)),
            pltpu.SemaphoreType.DMA,
        ],
        compiler_params=pltpu.CompilerParams(vmem_limit_bytes=60 << 20),
        cost_estimate=pl.CostEstimate(flops=0, bytes_accessed=5 << 20, transcendentals=0),
    )(send_to, jnp.asarray(np.argsort(COLUMN), jnp.int32), pages)


def around(place, step, sign):
    y = lax.rem(place // SIDE + SIDE + sign * (step // SIDE), SIDE)
    x = lax.rem(lax.rem(place, SIDE) + SIDE + sign * (step % SIDE), SIDE)
    return y * SIDE + x


def queries_kernel(where, queries, nope, rope, rows):
    rows[...] = queries[0, 0].astype(jnp.float32)
    for j in range(PEERS):
        ahead = pl.multiple_of(around(where[2], j, 1) * HEADS_PER, HEADS_PER)
        behind = pl.multiple_of(around(where[2], j, -1) * HEADS_PER, HEADS_PER)
        nope[j] = jnp.concatenate(
            [rows[t, pl.ds(ahead, HEADS_PER), :NOPE] for t in range(STEPS)], axis=0
        ).astype(jnp.bfloat16)
        rope[j * BLOCK : (j + 1) * BLOCK, :] = jnp.concatenate(
            [rows[t, pl.ds(behind, HEADS_PER), NOPE:] for t in range(STEPS)], axis=0
        ).astype(jnp.bfloat16)


def split_queries(where, queries):
    return pl.pallas_call(
        queries_kernel,
        out_shape=(
            jax.ShapeDtypeStruct((PEERS, BLOCK, NOPE), jnp.bfloat16),
            jax.ShapeDtypeStruct((ROWS, ROPE), jnp.bfloat16),
        ),
        grid_spec=pltpu.PrefetchScalarGridSpec(
            num_scalar_prefetch=1,
            grid=(1,),
            in_specs=[
                pl.BlockSpec((1,) + queries.shape[1:], lambda i, where: (where[1], 0, 0, 0, 0))
            ],
            out_specs=(
                pl.BlockSpec((PEERS, BLOCK, NOPE), lambda i, where: (0, 0, 0)),
                pl.BlockSpec((ROWS, ROPE), lambda i, where: (0, 0)),
            ),
            scratch_shapes=[pltpu.VMEM(queries.shape[2:], jnp.float32)],
        ),
        compiler_params=pltpu.CompilerParams(vmem_limit_bytes=8 << 20),
        cost_estimate=pl.CostEstimate(flops=0, bytes_accessed=600000, transcendentals=0),
    )(where, queries)


def absorb_kernel(where, heads, own, got, out):
    rows = heads[...]
    head = lax.rem(lax.broadcasted_iota(jnp.int32, rows.shape, 0), HEADS_PER)
    spread = jnp.concatenate(
        [jnp.where(head == h, rows, jnp.zeros_like(rows)) for h in range(HEADS_PER)], axis=1
    )
    for weight, half in ((own, where[1]), (got, 1 - where[1])):
        part = weight[0].reshape(HEADS_PER * NOPE, HALF)
        result = jnp.dot(spread, part, preferred_element_type=jnp.float32)
        result = result.astype(jnp.bfloat16)
        columns = pl.ds(pl.multiple_of(half * HALF, HALF), HALF)
        for j in range(PEERS):
            turned = (-(j // SIDE) % SIDE) * SIDE + -j % SIDE
            out[turned * BLOCK : (turned + 1) * BLOCK, columns] = result[j * BLOCK : (j + 1) * BLOCK]


def pick_values_kernel(where, own, got, out):
    layer = where[1]
    for weight, half in ((own, layer), (got, 1 - layer)):
        rows = pl.ds(pl.multiple_of(half * HALF, HALF), HALF)
        for h in range(HEADS_PER):
            out[h // 2, rows, h % 2 * VDIM : (h % 2 + 1) * VDIM] = weight[layer, h]


def pick_values(where, own, got):
    return pl.pallas_call(
        pick_values_kernel,
        out_shape=jax.ShapeDtypeStruct((HEADS_PER // 2 + 1, KV_RANK, 2 * VDIM), jnp.bfloat16),
        in_specs=[SMEM, VMEM, VMEM],
        out_specs=VMEM,
        compiler_params=pltpu.CompilerParams(vmem_limit_bytes=16 << 20),
        cost_estimate=pl.CostEstimate(flops=0, bytes_accessed=3 << 20, transcendentals=0),
    )(where, own, got)


def value_kernel(latent, weight, out):
    rows = latent[...]
    head = lax.rem(lax.broadcasted_iota(jnp.int32, (ROWS, VDIM), 0), HEADS_PER)
    result = jnp.zeros((ROWS, VDIM), jnp.float32)
    for p in range(HEADS_PER // 2):
        both = jnp.dot(rows, weight[p], preferred_element_type=jnp.float32)
        result = jnp.where(head == 2 * p, both[:, :VDIM], result)
        result = jnp.where(head == 2 * p + 1, both[:, VDIM:], result)
    result = result.astype(jnp.bfloat16)
    for k, place in enumerate(PLANE):
        out[place * BLOCK : (place + 1) * BLOCK, :] = result[k * BLOCK : (k + 1) * BLOCK]


def project_values(latent, weight):
    return pl.pallas_call(
        value_kernel,
        out_shape=jax.ShapeDtypeStruct((ROWS, VDIM), jnp.bfloat16),
        in_specs=[VMEM, VMEM],
        out_specs=VMEM,
        compiler_params=pltpu.CompilerParams(vmem_limit_bytes=16 << 20),
        cost_estimate=pl.CostEstimate(
            flops=2 * ROWS * 1024 * KV_RANK, bytes_accessed=2 << 20, transcendentals=0
        ),
    )(latent, weight)


def project(kernel, width, where, rows, own, got):
    shape = (1,) + own.shape[1:]
    weight_spec = pl.BlockSpec(shape, lambda i, where: (where[1], 0, 0, 0))
    return pl.pallas_call(
        kernel,
        out_shape=jax.ShapeDtypeStruct((ROWS, width), jnp.bfloat16),
        grid_spec=pltpu.PrefetchScalarGridSpec(
            num_scalar_prefetch=1,
            grid=(1,),
            in_specs=[pl.BlockSpec(rows.shape, lambda i, where: (0, 0)), weight_spec, weight_spec],
            out_specs=pl.BlockSpec((ROWS, width), lambda i, where: (0, 0)),
        ),
        compiler_params=pltpu.CompilerParams(vmem_limit_bytes=24 << 20),
        cost_estimate=pl.CostEstimate(
            flops=2 * ROWS * 1024 * KV_RANK, bytes_accessed=2 << 20, transcendentals=0
        ),
    )(where, rows, own, got)


def dot_rows(a, b):
    return lax.dot_general(a, b, (((1,), (1,)), ((), ())), preferred_element_type=jnp.float32)


def attend_kernel(where, inputs, pages, out, ropes, scores):
    for p in range(PEERS):
        for k in range(8):
            ropes[p * PAIR + 16 * k : p * PAIR + 16 * k + 16, :] = pages[
                p, PAIR:PAIR_ROWS, ROPE * k : ROPE * k + ROPE
            ]
    width = 4 * PAIR
    fresh = inputs[ROWS : ROWS + 16, :KV_RANK]
    fresh_rope = inputs[ROWS : ROWS + 16, KV_RANK : KV_RANK + ROPE]
    live = inputs[ROWS + 16 :, :PAIR].astype(jnp.float32) > 0.5

    def tile(first):
        rows = pl.ds(first, TILE)
        ql, qr = inputs[rows, :KV_RANK], inputs[rows, KV_RANK : KV_RANK + ROPE]
        row = lax.broadcasted_iota(jnp.int32, (TILE, 16), 0)
        key = lax.broadcasted_iota(jnp.int32, (TILE, 16), 1)
        extra = dot_rows(ql, fresh) + dot_rows(qr, fresh_rope)
        extra = jnp.where(key <= lax.rem(row // HEADS_PER, STEPS), extra, DEAD)
        highest = jnp.full((TILE, PAIR), DEAD, jnp.float32)
        for n in range(0, PEERS, 4):
            part = slice(n * PAIR, n * PAIR + width)
            lat = pages[n : n + 4, :PAIR, :].reshape(width, KV_RANK)
            s = dot_rows(ql, lat) + dot_rows(qr, ropes[part, :])
            bound = jnp.concatenate([live[p : p + 1] for p in range(n, n + 4)], axis=1)
            s = jnp.where(bound, s, DEAD)
            scores[:, part] = s
            for k in range(0, width, PAIR):
                highest = jnp.maximum(highest, s[:, k : k + PAIR])
        peak = jnp.maximum(
            jnp.max(extra, axis=1, keepdims=True), jnp.max(highest, axis=1, keepdims=True)
        )
        weight = jnp.exp2((extra - peak) * TO_LOG2).astype(jnp.bfloat16)
        total = jnp.sum(weight.astype(jnp.float32), axis=1, keepdims=True)
        summed = jnp.dot(weight, fresh, preferred_element_type=jnp.float32)
        added = jnp.zeros((TILE, PAIR), jnp.float32)
        for n in range(0, PEERS, 4):
            part = slice(n * PAIR, n * PAIR + width)
            lat = pages[n : n + 4, :PAIR, :].reshape(width, KV_RANK)
            weight = jnp.exp2((scores[:, part] - peak) * TO_LOG2).astype(jnp.bfloat16)
            kept = weight.astype(jnp.float32)
            for k in range(0, width, PAIR):
                added = added + kept[:, k : k + PAIR]
            summed = summed + jnp.dot(weight, lat, preferred_element_type=jnp.float32)
        total = total + jnp.sum(added, axis=1, keepdims=True)
        result = (summed * (1.0 / total)).astype(jnp.bfloat16)
        for k in range(TILE // BLOCK):
            rank = where[3 + around(where[2], first // BLOCK + k, -1)]
            out[rank] = result[k * BLOCK : (k + 1) * BLOCK]

    for first in range(0, ROWS, TILE):
        tile(first)


def attend(where, inputs, pages):
    keys = PEERS * PAIR
    return pl.pallas_call(
        attend_kernel,
        out_shape=jax.ShapeDtypeStruct((PEERS, BLOCK, KV_RANK), jnp.bfloat16),
        in_specs=[SMEM, VMEM, VMEM],
        out_specs=VMEM,
        scratch_shapes=[
            pltpu.VMEM((keys, ROPE), jnp.bfloat16),
            pltpu.VMEM((TILE, keys), jnp.float32),
        ],
        compiler_params=pltpu.CompilerParams(vmem_limit_bytes=40 << 20),
        cost_estimate=pl.CostEstimate(
            flops=2 * ROWS * keys * 1088, bytes_accessed=4 << 20, transcendentals=ROWS * keys
        ),
    )(where, inputs, pages)


def shifted(value, dy, dx):
    pairs = [
        (y * SIDE + x, ((y + dy) % SIDE) * SIDE + (x + dx) % SIDE)
        for y in range(SIDE)
        for x in range(SIDE)
    ]
    return lax.ppermute(value, "req", pairs)


def exchange(value):
    value = value.reshape((SIDE,) + (SIDE, BLOCK) + value.shape[1:])
    columns = [value[:, 0]] + [shifted(value[:, d], 0, d) for d in range(1, SIDE)]
    rows = jnp.stack(columns, axis=1)
    back = jnp.stack([rows[0]] + [shifted(rows[d], d, 0) for d in range(1, SIDE)])
    return back.reshape((ROWS,) + back.shape[3:])


def ordered_all_to_all(value, axis, order):
    return lax.all_to_all(
        value, axis, split_axis=0, concat_axis=0, tiled=True, axis_index_groups=[list(order)]
    )


def swapped(value):
    return lax.ppermute(value, "seq", [(0, 1), (1, 0)])


def shards(queries, w_absorb_k, w_absorb_v, prefill_pages, send_to, slot_of, lengths, new_latents):
    layer = lax.axis_index("seq")
    where = jnp.stack([lax.axis_index("group"), layer, lax.axis_index("req")]).astype(jnp.int32)
    where = jnp.concatenate([where, jnp.asarray(np.argsort(PLANE), jnp.int32)])

    sent = gather_pages(send_to[0, 0], prefill_pages[0, 0])
    pages = ordered_all_to_all(sent, ("group", "seq"), COLUMN)

    own_slot = slot_of[0, 0]
    nope, rope = split_queries(where, queries)
    heads = exchange(nope.reshape(ROWS, NOPE))
    latent = project(absorb_kernel, KV_RANK, where, heads, w_absorb_k, swapped(w_absorb_k))
    q_lat = exchange(latent)
    values = pick_values(where, w_absorb_v, swapped(w_absorb_v))

    fresh = lax.dynamic_index_in_dim(new_latents, layer, 0, keepdims=False)[0]
    slots = jnp.stack([own_slot, swapped(own_slot)])
    slots = jnp.where(layer == 0, slots, slots[::-1])
    starts = slots.T * PAGE + jnp.arange(2, dtype=jnp.int32) * BLOCK_KEYS
    live = starts[:, :, None] + jnp.arange(PAGE, dtype=jnp.int32) < lengths[0]
    inputs = jnp.concatenate(
        [
            jnp.concatenate([q_lat, rope, jnp.zeros_like(rope)], axis=1),
            jnp.pad(fresh, ((0, 16 - STEPS), (0, ROPE))),
            jnp.pad(
                live.reshape(PEERS, PAIR).astype(jnp.bfloat16)[np.array(COLUMN)],
                ((0, 0), (0, KV_RANK)),
            ),
        ]
    )
    inputs, values = lax.optimization_barrier((inputs, values))
    latent_out = attend(where, inputs, pages)
    latent_heads = ordered_all_to_all(latent_out, "req", PLANE)
    head_out = project_values(latent_heads.reshape(ROWS, KV_RANK), values)
    own = head_out.reshape(PEERS, STEPS, HEADS_PER, VDIM)
    got = swapped(own)
    return jnp.where(layer == 0, jnp.stack([own, got]), jnp.stack([got, own]))


def solution(mesh):
    in_specs = (
        P(None, ("group", "req"), None, None, None),
        P(None, "req", None, "seq"),
        P(None, "req", "seq", None),
        P(("group", "seq"), "req", None, None, None, None),
        P(("group", "seq"), "req", None),
        P(("group", "seq"), "req", None),
        P(("group", "req")),
        P(None, ("group", "req"), None, None),
    )
    out_specs = P(None, "group", None, "req", None)
    return jax.shard_map(shards, mesh=mesh, in_specs=in_specs, out_specs=out_specs, check_vma=False)
```

```python
import functools
import math

import jax
import jax.numpy as jnp
import numpy as np
from jax import lax
from jax.experimental import pallas as pl
from jax.experimental.pallas import tpu as pltpu
from jax.sharding import PartitionSpec as P

KV_RANK = 512
ROPE = 64
NOPE = 128
VDIM = 128
HEADS_PER = 8
STEPS = 4
PAGE = 64
PEERS = 16
BLOCK_KEYS = 1024
PAIR = 2 * PAGE
PAIR_ROWS = PAIR + 16
BLOCK = HEADS_PER * STEPS
ROWS = PEERS * BLOCK
TILE = 512
CHUNK = 2
COLUMN = (12, 15, 2, 1, 13, 0, 8, 6, 9, 7, 3, 4, 11, 10, 14, 5)
PLANE = (2, 13, 11, 3, 12, 0, 4, 7, 5, 14, 10, 6, 9, 8, 1, 15)
HALF = KV_RANK // 2
DEAD = -1e30
SCALE = 1.0 / math.sqrt(NOPE + ROPE)
TO_LOG2 = SCALE * math.log2(math.e)
SIDE = 4
VMEM = pl.BlockSpec(memory_space=pltpu.VMEM)
SMEM = pl.BlockSpec(memory_space=pltpu.SMEM)
ANY = pl.BlockSpec(memory_space=pl.ANY)


def send_kernel(send_to, order, pages, out, target_of, rank_of, held, packed, target_sem, in_sem, lat_sem, rope_sem):
    targets = pltpu.make_async_copy(send_to, target_of, target_sem.at[0])
    ranks = pltpu.make_async_copy(order, rank_of, target_sem.at[1])
    targets.start()
    ranks.start()

    def fetch(part):
        some = pl.ds(part * CHUNK, CHUNK)
        return pltpu.make_async_copy(pages.at[:, some], held.at[:, some], in_sem.at[part])

    def latents(layer, page):
        target = target_of[page]
        return pltpu.make_async_copy(
            held.at[layer, page, :, pl.ds(0, KV_RANK)],
            out.at[rank_of[target // 2 * 2 + layer], pl.ds(target % 2 * PAGE, PAGE)],
            lat_sem.at[layer, page],
        )

    for part in range(PEERS // CHUNK):
        fetch(part).start()
    targets.wait()
    ranks.wait()
    for part in range(PEERS // CHUNK):
        fetch(part).wait()
        for page in range(part * CHUNK, (part + 1) * CHUNK):
            for layer in range(2):
                latents(layer, page).start()
        for page in range(part * CHUNK, (part + 1) * CHUNK):
            target = target_of[page]
            columns = pl.ds(pl.multiple_of(target % 2 * (KV_RANK // 2), KV_RANK // 2), KV_RANK // 2)
            for layer in range(2):
                packed[rank_of[target // 2 * 2 + layer], :, columns] = jnp.concatenate(
                    [held[layer, page, 16 * k : 16 * k + 16, KV_RANK:] for k in range(PAGE // 16)],
                    axis=1,
                )
    ropes = pltpu.make_async_copy(packed, out.at[:, pl.ds(PAIR, 16)], rope_sem)
    ropes.start()
    for page in range(PEERS):
        for layer in range(2):
            latents(layer, page).wait()
    ropes.wait()


def gather_pages(send_to, pages):
    return pl.pallas_call(
        send_kernel,
        out_shape=jax.ShapeDtypeStruct((PEERS, PAIR_ROWS, KV_RANK), jnp.bfloat16),
        in_specs=[ANY, ANY, ANY],
        out_specs=ANY,
        scratch_shapes=[
            pltpu.SMEM((PEERS,), jnp.int32),
            pltpu.SMEM((PEERS,), jnp.int32),
            pltpu.VMEM(pages.shape, jnp.bfloat16),
            pltpu.VMEM((PEERS, 16, KV_RANK), jnp.bfloat16),
            pltpu.SemaphoreType.DMA((2,)),
            pltpu.SemaphoreType.DMA((PEERS // CHUNK,)),
            pltpu.SemaphoreType.DMA((2, PEERS)),
            pltpu.SemaphoreType.DMA,
        ],
        compiler_params=pltpu.CompilerParams(vmem_limit_bytes=60 << 20),
        cost_estimate=pl.CostEstimate(flops=0, bytes_accessed=5 << 20, transcendentals=0),
    )(send_to, jnp.asarray(np.argsort(COLUMN), jnp.int32), pages)


def around(place, step, sign):
    y = lax.rem(place // SIDE + SIDE + sign * (step // SIDE), SIDE)
    x = lax.rem(lax.rem(place, SIDE) + SIDE + sign * (step % SIDE), SIDE)
    return y * SIDE + x


def queries_kernel(where, queries, nope, rope, rows):
    rows[...] = queries[0, 0].astype(jnp.float32)
    for j in range(PEERS):
        ahead = pl.multiple_of(around(where[2], j, 1) * HEADS_PER, HEADS_PER)
        behind = pl.multiple_of(around(where[2], j, -1) * HEADS_PER, HEADS_PER)
        nope[j] = jnp.concatenate(
            [rows[t, pl.ds(ahead, HEADS_PER), :NOPE] for t in range(STEPS)], axis=0
        ).astype(jnp.bfloat16)
        rope[j * BLOCK : (j + 1) * BLOCK, :] = jnp.concatenate(
            [rows[t, pl.ds(behind, HEADS_PER), NOPE:] for t in range(STEPS)], axis=0
        ).astype(jnp.bfloat16)


def split_queries(where, queries):
    return pl.pallas_call(
        queries_kernel,
        out_shape=(
            jax.ShapeDtypeStruct((PEERS, BLOCK, NOPE), jnp.bfloat16),
            jax.ShapeDtypeStruct((ROWS, ROPE), jnp.bfloat16),
        ),
        grid_spec=pltpu.PrefetchScalarGridSpec(
            num_scalar_prefetch=1,
            grid=(1,),
            in_specs=[
                pl.BlockSpec((1,) + queries.shape[1:], lambda i, where: (where[1], 0, 0, 0, 0))
            ],
            out_specs=(
                pl.BlockSpec((PEERS, BLOCK, NOPE), lambda i, where: (0, 0, 0)),
                pl.BlockSpec((ROWS, ROPE), lambda i, where: (0, 0)),
            ),
            scratch_shapes=[pltpu.VMEM(queries.shape[2:], jnp.float32)],
        ),
        compiler_params=pltpu.CompilerParams(vmem_limit_bytes=8 << 20),
        cost_estimate=pl.CostEstimate(flops=0, bytes_accessed=600000, transcendentals=0),
    )(where, queries)


def absorb_kernel(where, heads, own, got, out):
    rows = heads[...]
    head = lax.rem(lax.broadcasted_iota(jnp.int32, rows.shape, 0), HEADS_PER)
    spread = jnp.concatenate(
        [jnp.where(head == h, rows, jnp.zeros_like(rows)) for h in range(HEADS_PER)], axis=1
    )
    for weight, half in ((own, where[1]), (got, 1 - where[1])):
        part = weight[0].reshape(HEADS_PER * NOPE, HALF)
        result = jnp.dot(spread, part, preferred_element_type=jnp.float32)
        result = result.astype(jnp.bfloat16)
        columns = pl.ds(pl.multiple_of(half * HALF, HALF), HALF)
        for j in range(PEERS):
            turned = (-(j // SIDE) % SIDE) * SIDE + -j % SIDE
            out[turned * BLOCK : (turned + 1) * BLOCK, columns] = result[j * BLOCK : (j + 1) * BLOCK]


def pick_values_kernel(where, own, got, out):
    layer = where[1]
    for weight, half in ((own, layer), (got, 1 - layer)):
        rows = pl.ds(pl.multiple_of(half * HALF, HALF), HALF)
        for h in range(HEADS_PER):
            out[h // 2, rows, h % 2 * VDIM : (h % 2 + 1) * VDIM] = weight[layer, h]


def pick_values(where, own, got):
    return pl.pallas_call(
        pick_values_kernel,
        out_shape=jax.ShapeDtypeStruct((HEADS_PER // 2 + 1, KV_RANK, 2 * VDIM), jnp.bfloat16),
        in_specs=[SMEM, VMEM, VMEM],
        out_specs=VMEM,
        compiler_params=pltpu.CompilerParams(vmem_limit_bytes=16 << 20),
        cost_estimate=pl.CostEstimate(flops=0, bytes_accessed=3 << 20, transcendentals=0),
    )(where, own, got)


def value_kernel(latent, weight, out):
    rows = latent[...]
    head = lax.rem(lax.broadcasted_iota(jnp.int32, (ROWS, VDIM), 0), HEADS_PER)
    result = jnp.zeros((ROWS, VDIM), jnp.float32)
    for p in range(HEADS_PER // 2):
        both = jnp.dot(rows, weight[p], preferred_element_type=jnp.float32)
        result = jnp.where(head == 2 * p, both[:, :VDIM], result)
        result = jnp.where(head == 2 * p + 1, both[:, VDIM:], result)
    result = result.astype(jnp.bfloat16)
    for k, place in enumerate(PLANE):
        out[place * BLOCK : (place + 1) * BLOCK, :] = result[k * BLOCK : (k + 1) * BLOCK]


def project_values(latent, weight):
    return pl.pallas_call(
        value_kernel,
        out_shape=jax.ShapeDtypeStruct((ROWS, VDIM), jnp.bfloat16),
        in_specs=[VMEM, VMEM],
        out_specs=VMEM,
        compiler_params=pltpu.CompilerParams(vmem_limit_bytes=16 << 20),
        cost_estimate=pl.CostEstimate(
            flops=2 * ROWS * 1024 * KV_RANK, bytes_accessed=2 << 20, transcendentals=0
        ),
    )(latent, weight)


def project(kernel, width, where, rows, own, got):
    shape = (1,) + own.shape[1:]
    weight_spec = pl.BlockSpec(shape, lambda i, where: (where[1], 0, 0, 0))
    return pl.pallas_call(
        kernel,
        out_shape=jax.ShapeDtypeStruct((ROWS, width), jnp.bfloat16),
        grid_spec=pltpu.PrefetchScalarGridSpec(
            num_scalar_prefetch=1,
            grid=(1,),
            in_specs=[pl.BlockSpec(rows.shape, lambda i, where: (0, 0)), weight_spec, weight_spec],
            out_specs=pl.BlockSpec((ROWS, width), lambda i, where: (0, 0)),
        ),
        compiler_params=pltpu.CompilerParams(vmem_limit_bytes=24 << 20),
        cost_estimate=pl.CostEstimate(
            flops=2 * ROWS * 1024 * KV_RANK, bytes_accessed=2 << 20, transcendentals=0
        ),
    )(where, rows, own, got)


def dot_rows(a, b):
    return lax.dot_general(a, b, (((1,), (1,)), ((), ())), preferred_element_type=jnp.float32)


def attend_kernel(where, inputs, pages, out, ropes, scores):
    for p in range(PEERS):
        for k in range(8):
            ropes[p * PAIR + 16 * k : p * PAIR + 16 * k + 16, :] = pages[
                p, PAIR:PAIR_ROWS, ROPE * k : ROPE * k + ROPE
            ]
    width = 4 * PAIR
    fresh = inputs[ROWS : ROWS + 16, :KV_RANK]
    fresh_rope = inputs[ROWS : ROWS + 16, KV_RANK : KV_RANK + ROPE]
    live = inputs[ROWS + 16 :, :PAIR].astype(jnp.float32) > 0.5

    def tile(first):
        rows = pl.ds(first, TILE)
        ql, qr = inputs[rows, :KV_RANK], inputs[rows, KV_RANK : KV_RANK + ROPE]
        row = lax.broadcasted_iota(jnp.int32, (TILE, 16), 0)
        key = lax.broadcasted_iota(jnp.int32, (TILE, 16), 1)
        extra = dot_rows(ql, fresh) + dot_rows(qr, fresh_rope)
        extra = jnp.where(key <= lax.rem(row // HEADS_PER, STEPS), extra, DEAD)
        highest = jnp.full((TILE, PAIR), DEAD, jnp.float32)
        for n in range(0, PEERS, 4):
            part = slice(n * PAIR, n * PAIR + width)
            lat = pages[n : n + 4, :PAIR, :].reshape(width, KV_RANK)
            s = dot_rows(ql, lat) + dot_rows(qr, ropes[part, :])
            bound = jnp.concatenate([live[p : p + 1] for p in range(n, n + 4)], axis=1)
            s = jnp.where(bound, s, DEAD)
            scores[:, part] = s
            for k in range(0, width, PAIR):
                highest = jnp.maximum(highest, s[:, k : k + PAIR])
        peak = jnp.maximum(
            jnp.max(extra, axis=1, keepdims=True), jnp.max(highest, axis=1, keepdims=True)
        )
        weight = jnp.exp2((extra - peak) * TO_LOG2).astype(jnp.bfloat16)
        total = jnp.sum(weight.astype(jnp.float32), axis=1, keepdims=True)
        summed = jnp.dot(weight, fresh, preferred_element_type=jnp.float32)
        added = jnp.zeros((TILE, PAIR), jnp.float32)
        for n in range(0, PEERS, 4):
            part = slice(n * PAIR, n * PAIR + width)
            lat = pages[n : n + 4, :PAIR, :].reshape(width, KV_RANK)
            weight = jnp.exp2((scores[:, part] - peak) * TO_LOG2).astype(jnp.bfloat16)
            kept = weight.astype(jnp.float32)
            for k in range(0, width, PAIR):
                added = added + kept[:, k : k + PAIR]
            summed = summed + jnp.dot(weight, lat, preferred_element_type=jnp.float32)
        total = total + jnp.sum(added, axis=1, keepdims=True)
        result = (summed * (1.0 / total)).astype(jnp.bfloat16)
        for k in range(TILE // BLOCK):
            rank = where[3 + around(where[2], first // BLOCK + k, -1)]
            out[rank] = result[k * BLOCK : (k + 1) * BLOCK]

    for first in range(0, ROWS, TILE):
        tile(first)


def attend(where, inputs, pages):
    keys = PEERS * PAIR
    return pl.pallas_call(
        attend_kernel,
        out_shape=jax.ShapeDtypeStruct((PEERS, BLOCK, KV_RANK), jnp.bfloat16),
        in_specs=[SMEM, VMEM, VMEM],
        out_specs=VMEM,
        scratch_shapes=[
            pltpu.VMEM((keys, ROPE), jnp.bfloat16),
            pltpu.VMEM((TILE, keys), jnp.float32),
        ],
        compiler_params=pltpu.CompilerParams(vmem_limit_bytes=40 << 20),
        cost_estimate=pl.CostEstimate(
            flops=2 * ROWS * keys * 1088, bytes_accessed=4 << 20, transcendentals=ROWS * keys
        ),
    )(where, inputs, pages)


def shifted(value, dy, dx):
    pairs = [
        (y * SIDE + x, ((y + dy) % SIDE) * SIDE + (x + dx) % SIDE)
        for y in range(SIDE)
        for x in range(SIDE)
    ]
    return lax.ppermute(value, "req", pairs)


def exchange(value):
    value = value.reshape((SIDE,) + (SIDE, BLOCK) + value.shape[1:])
    columns = [value[:, 0]] + [shifted(value[:, d], 0, d) for d in range(1, SIDE)]
    rows = jnp.stack(columns, axis=1)
    back = jnp.stack([rows[0]] + [shifted(rows[d], d, 0) for d in range(1, SIDE)])
    return back.reshape((ROWS,) + back.shape[3:])


def ordered_all_to_all(value, axis, order):
    return lax.all_to_all(
        value, axis, split_axis=0, concat_axis=0, tiled=True, axis_index_groups=[list(order)]
    )


def swapped(value):
    return lax.ppermute(value, "seq", [(0, 1), (1, 0)])


def shards(queries, w_absorb_k, w_absorb_v, prefill_pages, send_to, slot_of, lengths, new_latents):
    layer = lax.axis_index("seq")
    where = jnp.stack([lax.axis_index("group"), layer, lax.axis_index("req")]).astype(jnp.int32)
    where = jnp.concatenate([where, jnp.asarray(np.argsort(PLANE), jnp.int32)])

    sent = gather_pages(send_to[0, 0], prefill_pages[0, 0])
    pages = ordered_all_to_all(sent, ("group", "seq"), COLUMN)

    own_slot = slot_of[0, 0]
    nope, rope = split_queries(where, queries)
    heads = exchange(nope.reshape(ROWS, NOPE))
    latent = project(absorb_kernel, KV_RANK, where, heads, w_absorb_k, swapped(w_absorb_k))
    q_lat = exchange(latent)
    values = pick_values(where, w_absorb_v, swapped(w_absorb_v))

    fresh = lax.dynamic_index_in_dim(new_latents, layer, 0, keepdims=False)[0]
    slots = jnp.stack([own_slot, swapped(own_slot)])
    slots = jnp.where(layer == 0, slots, slots[::-1])
    starts = slots.T * PAGE + jnp.arange(2, dtype=jnp.int32) * BLOCK_KEYS
    live = starts[:, :, None] + jnp.arange(PAGE, dtype=jnp.int32) < lengths[0]
    inputs = jnp.concatenate(
        [
            jnp.concatenate([q_lat, rope, jnp.zeros_like(rope)], axis=1),
            jnp.pad(fresh, ((0, 16 - STEPS), (0, ROPE))),
            jnp.pad(
                live.reshape(PEERS, PAIR).astype(jnp.bfloat16)[np.array(COLUMN)],
                ((0, 0), (0, KV_RANK)),
            ),
        ]
    )
    inputs, values = lax.optimization_barrier((inputs, values))
    latent_out = attend(where, inputs, pages)
    latent_heads = ordered_all_to_all(latent_out, "req", PLANE)
    head_out = project_values(latent_heads.reshape(ROWS, KV_RANK), values)
    own = head_out.reshape(PEERS, STEPS, HEADS_PER, VDIM)
    got = swapped(own)
    return jnp.where(layer == 0, jnp.stack([own, got]), jnp.stack([got, own]))


def solution(mesh):
    in_specs = (
        P(None, ("group", "req"), None, None, None),
        P(None, "req", None, "seq"),
        P(None, "req", "seq", None),
        P(("group", "seq"), "req", None, None, None, None),
        P(("group", "seq"), "req", None),
        P(("group", "seq"), "req", None),
        P(("group", "req")),
        P(None, ("group", "req"), None, None),
    )
    out_specs = P(None, "group", None, "req", None)
    return jax.shard_map(shards, mesh=mesh, in_specs=in_specs, out_specs=out_specs, check_vma=False)
```

```python
import functools
import math

import jax
import jax.numpy as jnp
import numpy as np
from jax import lax
from jax.experimental import pallas as pl
from jax.experimental.pallas import tpu as pltpu
from jax.sharding import PartitionSpec as P

KV_RANK = 512
ROPE = 64
NOPE = 128
VDIM = 128
HEADS_PER = 8
STEPS = 4
PAGE = 64
PEERS = 16
BLOCK_KEYS = 1024
PAIR = 2 * PAGE
PAIR_ROWS = PAIR + 16
BLOCK = HEADS_PER * STEPS
ROWS = PEERS * BLOCK
TILE = 512
CHUNK = 1
COLUMN = (12, 15, 2, 1, 13, 0, 8, 6, 9, 7, 3, 4, 11, 10, 14, 5)
PLANE = (2, 13, 11, 3, 12, 0, 4, 7, 5, 14, 10, 6, 9, 8, 1, 15)
HALF = KV_RANK // 2
DEAD = -1e30
SCALE = 1.0 / math.sqrt(NOPE + ROPE)
TO_LOG2 = SCALE * math.log2(math.e)
SIDE = 4
VMEM = pl.BlockSpec(memory_space=pltpu.VMEM)
SMEM = pl.BlockSpec(memory_space=pltpu.SMEM)
ANY = pl.BlockSpec(memory_space=pl.ANY)


def send_kernel(send_to, order, pages, out, target_of, rank_of, held, packed, target_sem, in_sem, lat_sem, rope_sem):
    targets = pltpu.make_async_copy(send_to, target_of, target_sem.at[0])
    ranks = pltpu.make_async_copy(order, rank_of, target_sem.at[1])
    targets.start()
    ranks.start()

    def fetch(part):
        some = pl.ds(part * CHUNK, CHUNK)
        return pltpu.make_async_copy(pages.at[:, some], held.at[:, some], in_sem.at[part])

    def latents(layer, page):
        target = target_of[page]
        return pltpu.make_async_copy(
            held.at[layer, page, :, pl.ds(0, KV_RANK)],
            out.at[rank_of[target // 2 * 2 + layer], pl.ds(target % 2 * PAGE, PAGE)],
            lat_sem.at[layer, page],
        )

    for part in range(PEERS // CHUNK):
        fetch(part).start()
    targets.wait()
    ranks.wait()
    for part in range(PEERS // CHUNK):
        fetch(part).wait()
        for page in range(part * CHUNK, (part + 1) * CHUNK):
            for layer in range(2):
                latents(layer, page).start()
        for page in range(part * CHUNK, (part + 1) * CHUNK):
            target = target_of[page]
            columns = pl.ds(pl.multiple_of(target % 2 * (KV_RANK // 2), KV_RANK // 2), KV_RANK // 2)
            for layer in range(2):
                packed[rank_of[target // 2 * 2 + layer], :, columns] = jnp.concatenate(
                    [held[layer, page, 16 * k : 16 * k + 16, KV_RANK:] for k in range(PAGE // 16)],
                    axis=1,
                )
    ropes = pltpu.make_async_copy(packed, out.at[:, pl.ds(PAIR, 16)], rope_sem)
    ropes.start()
    for page in range(PEERS):
        for layer in range(2):
            latents(layer, page).wait()
    ropes.wait()


def gather_pages(send_to, pages):
    return pl.pallas_call(
        send_kernel,
        out_shape=jax.ShapeDtypeStruct((PEERS, PAIR_ROWS, KV_RANK), jnp.bfloat16),
        in_specs=[ANY, ANY, ANY],
        out_specs=ANY,
        scratch_shapes=[
            pltpu.SMEM((PEERS,), jnp.int32),
            pltpu.SMEM((PEERS,), jnp.int32),
            pltpu.VMEM(pages.shape, jnp.bfloat16),
            pltpu.VMEM((PEERS, 16, KV_RANK), jnp.bfloat16),
            pltpu.SemaphoreType.DMA((2,)),
            pltpu.SemaphoreType.DMA((PEERS // CHUNK,)),
            pltpu.SemaphoreType.DMA((2, PEERS)),
            pltpu.SemaphoreType.DMA,
        ],
        compiler_params=pltpu.CompilerParams(vmem_limit_bytes=60 << 20),
        cost_estimate=pl.CostEstimate(flops=0, bytes_accessed=5 << 20, transcendentals=0),
    )(send_to, jnp.asarray(np.argsort(COLUMN), jnp.int32), pages)


def around(place, step, sign):
    y = lax.rem(place // SIDE + SIDE + sign * (step // SIDE), SIDE)
    x = lax.rem(lax.rem(place, SIDE) + SIDE + sign * (step % SIDE), SIDE)
    return y * SIDE + x


def queries_kernel(where, queries, nope, rope, rows):
    rows[...] = queries[0, 0].astype(jnp.float32)
    for j in range(PEERS):
        ahead = pl.multiple_of(around(where[2], j, 1) * HEADS_PER, HEADS_PER)
        behind = pl.multiple_of(around(where[2], j, -1) * HEADS_PER, HEADS_PER)
        nope[j] = jnp.concatenate(
            [rows[t, pl.ds(ahead, HEADS_PER), :NOPE] for t in range(STEPS)], axis=0
        ).astype(jnp.bfloat16)
        rope[j * BLOCK : (j + 1) * BLOCK, :] = jnp.concatenate(
            [rows[t, pl.ds(behind, HEADS_PER), NOPE:] for t in range(STEPS)], axis=0
        ).astype(jnp.bfloat16)


def split_queries(where, queries):
    return pl.pallas_call(
        queries_kernel,
        out_shape=(
            jax.ShapeDtypeStruct((PEERS, BLOCK, NOPE), jnp.bfloat16),
            jax.ShapeDtypeStruct((ROWS, ROPE), jnp.bfloat16),
        ),
        grid_spec=pltpu.PrefetchScalarGridSpec(
            num_scalar_prefetch=1,
            grid=(1,),
            in_specs=[
                pl.BlockSpec((1,) + queries.shape[1:], lambda i, where: (where[1], 0, 0, 0, 0))
            ],
            out_specs=(
                pl.BlockSpec((PEERS, BLOCK, NOPE), lambda i, where: (0, 0, 0)),
                pl.BlockSpec((ROWS, ROPE), lambda i, where: (0, 0)),
            ),
            scratch_shapes=[pltpu.VMEM(queries.shape[2:], jnp.float32)],
        ),
        compiler_params=pltpu.CompilerParams(vmem_limit_bytes=8 << 20),
        cost_estimate=pl.CostEstimate(flops=0, bytes_accessed=600000, transcendentals=0),
    )(where, queries)


def absorb_kernel(where, heads, own, got, out):
    rows = heads[...]
    head = lax.rem(lax.broadcasted_iota(jnp.int32, rows.shape, 0), HEADS_PER)
    spread = jnp.concatenate(
        [jnp.where(head == h, rows, jnp.zeros_like(rows)) for h in range(HEADS_PER)], axis=1
    )
    for weight, half in ((own, where[1]), (got, 1 - where[1])):
        part = weight[0].reshape(HEADS_PER * NOPE, HALF)
        result = jnp.dot(spread, part, preferred_element_type=jnp.float32)
        result = result.astype(jnp.bfloat16)
        columns = pl.ds(pl.multiple_of(half * HALF, HALF), HALF)
        for j in range(PEERS):
            turned = (-(j // SIDE) % SIDE) * SIDE + -j % SIDE
            out[turned * BLOCK : (turned + 1) * BLOCK, columns] = result[j * BLOCK : (j + 1) * BLOCK]


def pick_values_kernel(where, own, got, out):
    layer = where[1]
    for weight, half in ((own, layer), (got, 1 - layer)):
        rows = pl.ds(pl.multiple_of(half * HALF, HALF), HALF)
        for h in range(HEADS_PER):
            out[h // 2, rows, h % 2 * VDIM : (h % 2 + 1) * VDIM] = weight[layer, h]


def pick_values(where, own, got):
    return pl.pallas_call(
        pick_values_kernel,
        out_shape=jax.ShapeDtypeStruct((HEADS_PER // 2 + 1, KV_RANK, 2 * VDIM), jnp.bfloat16),
        in_specs=[SMEM, VMEM, VMEM],
        out_specs=VMEM,
        compiler_params=pltpu.CompilerParams(vmem_limit_bytes=16 << 20),
        cost_estimate=pl.CostEstimate(flops=0, bytes_accessed=3 << 20, transcendentals=0),
    )(where, own, got)


def value_kernel(latent, weight, out):
    rows = latent[...]
    head = lax.rem(lax.broadcasted_iota(jnp.int32, (ROWS, VDIM), 0), HEADS_PER)
    result = jnp.zeros((ROWS, VDIM), jnp.float32)
    for p in range(HEADS_PER // 2):
        both = jnp.dot(rows, weight[p], preferred_element_type=jnp.float32)
        result = jnp.where(head == 2 * p, both[:, :VDIM], result)
        result = jnp.where(head == 2 * p + 1, both[:, VDIM:], result)
    result = result.astype(jnp.bfloat16)
    for k, place in enumerate(PLANE):
        out[place * BLOCK : (place + 1) * BLOCK, :] = result[k * BLOCK : (k + 1) * BLOCK]


def project_values(latent, weight):
    return pl.pallas_call(
        value_kernel,
        out_shape=jax.ShapeDtypeStruct((ROWS, VDIM), jnp.bfloat16),
        in_specs=[VMEM, VMEM],
        out_specs=VMEM,
        compiler_params=pltpu.CompilerParams(vmem_limit_bytes=16 << 20),
        cost_estimate=pl.CostEstimate(
            flops=2 * ROWS * 1024 * KV_RANK, bytes_accessed=2 << 20, transcendentals=0
        ),
    )(latent, weight)


def project(kernel, width, where, rows, own, got):
    shape = (1,) + own.shape[1:]
    weight_spec = pl.BlockSpec(shape, lambda i, where: (where[1], 0, 0, 0))
    return pl.pallas_call(
        kernel,
        out_shape=jax.ShapeDtypeStruct((ROWS, width), jnp.bfloat16),
        grid_spec=pltpu.PrefetchScalarGridSpec(
            num_scalar_prefetch=1,
            grid=(1,),
            in_specs=[pl.BlockSpec(rows.shape, lambda i, where: (0, 0)), weight_spec, weight_spec],
            out_specs=pl.BlockSpec((ROWS, width), lambda i, where: (0, 0)),
        ),
        compiler_params=pltpu.CompilerParams(vmem_limit_bytes=24 << 20),
        cost_estimate=pl.CostEstimate(
            flops=2 * ROWS * 1024 * KV_RANK, bytes_accessed=2 << 20, transcendentals=0
        ),
    )(where, rows, own, got)


def dot_rows(a, b):
    return lax.dot_general(a, b, (((1,), (1,)), ((), ())), preferred_element_type=jnp.float32)


def attend_kernel(where, inputs, pages, out, ropes, scores):
    for p in range(PEERS):
        for k in range(8):
            ropes[p * PAIR + 16 * k : p * PAIR + 16 * k + 16, :] = pages[
                p, PAIR:PAIR_ROWS, ROPE * k : ROPE * k + ROPE
            ]
    width = 4 * PAIR
    fresh = inputs[ROWS : ROWS + 16, :KV_RANK]
    fresh_rope = inputs[ROWS : ROWS + 16, KV_RANK : KV_RANK + ROPE]
    live = inputs[ROWS + 16 :, :PAIR].astype(jnp.float32) > 0.5

    def tile(first):
        rows = pl.ds(first, TILE)
        ql, qr = inputs[rows, :KV_RANK], inputs[rows, KV_RANK : KV_RANK + ROPE]
        row = lax.broadcasted_iota(jnp.int32, (TILE, 16), 0)
        key = lax.broadcasted_iota(jnp.int32, (TILE, 16), 1)
        extra = dot_rows(ql, fresh) + dot_rows(qr, fresh_rope)
        extra = jnp.where(key <= lax.rem(row // HEADS_PER, STEPS), extra, DEAD)
        highest = jnp.full((TILE, PAIR), DEAD, jnp.float32)
        for n in range(0, PEERS, 4):
            part = slice(n * PAIR, n * PAIR + width)
            lat = pages[n : n + 4, :PAIR, :].reshape(width, KV_RANK)
            s = dot_rows(ql, lat) + dot_rows(qr, ropes[part, :])
            bound = jnp.concatenate([live[p : p + 1] for p in range(n, n + 4)], axis=1)
            s = jnp.where(bound, s, DEAD)
            scores[:, part] = s
            for k in range(0, width, PAIR):
                highest = jnp.maximum(highest, s[:, k : k + PAIR])
        peak = jnp.maximum(
            jnp.max(extra, axis=1, keepdims=True), jnp.max(highest, axis=1, keepdims=True)
        )
        weight = jnp.exp2((extra - peak) * TO_LOG2).astype(jnp.bfloat16)
        total = jnp.sum(weight.astype(jnp.float32), axis=1, keepdims=True)
        summed = jnp.dot(weight, fresh, preferred_element_type=jnp.float32)
        added = jnp.zeros((TILE, PAIR), jnp.float32)
        for n in range(0, PEERS, 4):
            part = slice(n * PAIR, n * PAIR + width)
            lat = pages[n : n + 4, :PAIR, :].reshape(width, KV_RANK)
            weight = jnp.exp2((scores[:, part] - peak) * TO_LOG2).astype(jnp.bfloat16)
            kept = weight.astype(jnp.float32)
            for k in range(0, width, PAIR):
                added = added + kept[:, k : k + PAIR]
            summed = summed + jnp.dot(weight, lat, preferred_element_type=jnp.float32)
        total = total + jnp.sum(added, axis=1, keepdims=True)
        result = (summed * (1.0 / total)).astype(jnp.bfloat16)
        for k in range(TILE // BLOCK):
            rank = where[3 + around(where[2], first // BLOCK + k, -1)]
            out[rank] = result[k * BLOCK : (k + 1) * BLOCK]

    for first in range(0, ROWS, TILE):
        tile(first)


def attend(where, inputs, pages):
    keys = PEERS * PAIR
    return pl.pallas_call(
        attend_kernel,
        out_shape=jax.ShapeDtypeStruct((PEERS, BLOCK, KV_RANK), jnp.bfloat16),
        in_specs=[SMEM, VMEM, VMEM],
        out_specs=VMEM,
        scratch_shapes=[
            pltpu.VMEM((keys, ROPE), jnp.bfloat16),
            pltpu.VMEM((TILE, keys), jnp.float32),
        ],
        compiler_params=pltpu.CompilerParams(vmem_limit_bytes=40 << 20),
        cost_estimate=pl.CostEstimate(
            flops=2 * ROWS * keys * 1088, bytes_accessed=4 << 20, transcendentals=ROWS * keys
        ),
    )(where, inputs, pages)


def shifted(value, dy, dx):
    pairs = [
        (y * SIDE + x, ((y + dy) % SIDE) * SIDE + (x + dx) % SIDE)
        for y in range(SIDE)
        for x in range(SIDE)
    ]
    return lax.ppermute(value, "req", pairs)


def exchange(value):
    value = value.reshape((SIDE,) + (SIDE, BLOCK) + value.shape[1:])
    columns = [value[:, 0]] + [shifted(value[:, d], 0, d) for d in range(1, SIDE)]
    rows = jnp.stack(columns, axis=1)
    back = jnp.stack([rows[0]] + [shifted(rows[d], d, 0) for d in range(1, SIDE)])
    return back.reshape((ROWS,) + back.shape[3:])


def ordered_all_to_all(value, axis, order):
    return lax.all_to_all(
        value, axis, split_axis=0, concat_axis=0, tiled=True, axis_index_groups=[list(order)]
    )


def swapped(value):
    return lax.ppermute(value, "seq", [(0, 1), (1, 0)])


def shards(queries, w_absorb_k, w_absorb_v, prefill_pages, send_to, slot_of, lengths, new_latents):
    layer = lax.axis_index("seq")
    where = jnp.stack([lax.axis_index("group"), layer, lax.axis_index("req")]).astype(jnp.int32)
    where = jnp.concatenate([where, jnp.asarray(np.argsort(PLANE), jnp.int32)])

    sent = gather_pages(send_to[0, 0], prefill_pages[0, 0])
    pages = ordered_all_to_all(sent, ("group", "seq"), COLUMN)

    own_slot = slot_of[0, 0]
    nope, rope = split_queries(where, queries)
    heads = exchange(nope.reshape(ROWS, NOPE))
    latent = project(absorb_kernel, KV_RANK, where, heads, w_absorb_k, swapped(w_absorb_k))
    q_lat = exchange(latent)
    values = pick_values(where, w_absorb_v, swapped(w_absorb_v))

    fresh = lax.dynamic_index_in_dim(new_latents, layer, 0, keepdims=False)[0]
    slots = jnp.stack([own_slot, swapped(own_slot)])
    slots = jnp.where(layer == 0, slots, slots[::-1])
    starts = slots.T * PAGE + jnp.arange(2, dtype=jnp.int32) * BLOCK_KEYS
    live = starts[:, :, None] + jnp.arange(PAGE, dtype=jnp.int32) < lengths[0]
    inputs = jnp.concatenate(
        [
            jnp.concatenate([q_lat, rope, jnp.zeros_like(rope)], axis=1),
            jnp.pad(fresh, ((0, 16 - STEPS), (0, ROPE))),
            jnp.pad(
                live.reshape(PEERS, PAIR).astype(jnp.bfloat16)[np.array(COLUMN)],
                ((0, 0), (0, KV_RANK)),
            ),
        ]
    )
    inputs, values = lax.optimization_barrier((inputs, values))
    latent_out = attend(where, inputs, pages)
    latent_heads = ordered_all_to_all(latent_out, "req", PLANE)
    head_out = project_values(latent_heads.reshape(ROWS, KV_RANK), values)
    own = head_out.reshape(PEERS, STEPS, HEADS_PER, VDIM)
    got = swapped(own)
    return jnp.where(layer == 0, jnp.stack([own, got]), jnp.stack([got, own]))


def solution(mesh):
    in_specs = (
        P(None, ("group", "req"), None, None, None),
        P(None, "req", None, "seq"),
        P(None, "req", "seq", None),
        P(("group", "seq"), "req", None, None, None, None),
        P(("group", "seq"), "req", None),
        P(("group", "seq"), "req", None),
        P(("group", "req")),
        P(None, ("group", "req"), None, None),
    )
    out_specs = P(None, "group", None, "req", None)
    return jax.shard_map(shards, mesh=mesh, in_specs=in_specs, out_specs=out_specs, check_vma=False)
```
